512 devices in a mesh: ens: 16 (over x, y), tile: 32 (over z, core).
Axes of the slice: x: 4, y: 4, z: 16, core: 2. Of those that a mesh axis runs over, the one named last changes fastest.
Arguments:
- air_latent_array: bfloat16 [16, 32, 64, 384], P('ens', 'tile'), may hold values from -6 to 6
- air_exchange_projection: bfloat16 [384, 128], replicated, may hold values from -0.3125 to 0.3125
- marine_latent_array: bfloat16 [16, 128, 256, 256], P('ens', None, 'tile'), may hold values from -6 to 6
- driver_projection_matrix: bfloat16 [128, 256], replicated, may hold values from -0.5 to 0.5
- spatial_kernel_taps: float32 [9, 256], replicated, may hold values from -1.5 to 1.5
- layernorm_multiplier: float32 [256], replicated, may hold values from 0.25 to 1.75
- pointwise_widen_matrix: bfloat16 [256, 1024], replicated, may hold values from -0.375 to 0.375
- pointwise_shrink_matrix: bfloat16 [1024, 256], replicated, may hold values from -0.1875 to 0.1875
- thermal_projection_matrix: bfloat16 [256, 128], replicated, may hold values from -0.375 to 0.375
- intersecting_air_sites: int32 [4, 128, 256], P(None, None, 'tile'), may hold values from 0 to 63, as said below
- margin_multiplier: int32 [4, 128, 256], P(None, None, 'tile'), may hold values from 1 to 8
- terrain_water_indicator: int32 [128, 256], P(None, 'tile'), may hold values from 0 to 1, as said below
- marine_successor_adjoint: bfloat16 [16, 128, 256, 256], P('ens', None, 'tile'), may hold values from -6 to 6
Outputs:
- marine_successor_latent: bfloat16 [16, 128, 256, 256], P('ens', None, 'tile')
- sst_atm: bfloat16 [16, 32, 64, 128], P('ens', 'tile')
- marine_latent_adjoint: bfloat16 [16, 128, 256, 256], P('ens', None, 'tile')
- grad_force: bfloat16 [128, 256], replicated
- grad_conv: bfloat16 [9, 256], replicated
- grad_gain: bfloat16 [256], replicated
- grad_up: bfloat16 [256, 1024], replicated
- grad_down: bfloat16 [1024, 256], replicated
The draws below stay inside these ranges and needn't reach their ends.
Inputs may be any that keep to these rules, and one draw needn't show every extreme that they name: `intersecting_air_sites`: the index of an atmosphere cell that lies over the ocean cell's own tile: row * 2 + column, with the row among all 32 rows and the column among the 2 atmosphere columns over that tile. `terrain_water_indicator`: 1 marks a sea cell, 0 a land cell.
All inputs are finite; a program needn't handle non-finite values.
Results may differ from the reference program's by a relative error of at most 0.0082.
Values may be sent and summed in bfloat16 or wider, within the bound.
No kernel may reach another device: no remote copies, remote signals or barrier semaphores. Data moves between devices by JAX's collectives and lax.ppermute only.
A program may use at most 64 MiB of HBM per device.

```python
import math
import jax
import jax.numpy as jnp
from jax import lax

ACOLS = 2
SUBDIVISION = 4
K = 4
KS = 3
MARINE_DIMENSION = 256
HID = 1024
AW = 384
LINKED_QUANTITY = 128
MEMBERS = 16
ALAT = 32
ALON = 64
OLAT = 128
OCOLS = 8
OLON = 256


def draw_intersecting_air_sites(key, part):
    first_key, second_key = jax.random.split(key)
    base_rows = (jnp.arange(OLAT) // SUBDIVISION).astype(jnp.int32)[None, :, None]
    base_cols = (jnp.arange(OLON) % OCOLS // SUBDIVISION).astype(jnp.int32)[None, None, :]
    row_shift = jax.random.randint(first_key, (K, OLAT, OLON), -1, 2)
    col_shift = jax.random.randint(second_key, (K, OLAT, OLON), -1, 2)
    leading = (jnp.arange(K) == 0)[:, None, None]
    row_shift = jnp.where(leading, 0, row_shift)
    col_shift = jnp.where(leading, 0, col_shift)
    rows = jnp.clip(base_rows + row_shift, 0, ALAT - 1)
    cols = jnp.clip(base_cols + col_shift, 0, ACOLS - 1)
    return (rows * ACOLS + cols).astype(jnp.int32)


def draw_terrain_water_indicator(key, part):
    level_key, coarse_key, fine_key = jax.random.split(key, 3)
    strips = OLON // OCOLS
    level = jax.random.randint(level_key, (strips,), 1, 5)
    column_level = level[jnp.arange(ALON) // ACOLS]
    coarse = jax.random.randint(coarse_key, (ALAT, ALON), 0, 4) < column_level[None, :]
    coarse_fine = jnp.repeat(jnp.repeat(coarse, SUBDIVISION, axis=0), SUBDIVISION, axis=1)
    fine = jax.random.randint(fine_key, (OLAT, OLON), 0, 8) < 7
    return (coarse_fine & fine).astype(jnp.int32)


def plant(drawn, rng, smallest, top_value):
    dims = drawn.shape
    place = [jax.random.randint(jax.random.fold_in(rng, axis), (), 0, dims[axis]) for axis in range(len(dims))]
    drawn = drawn.at[tuple(place)].set(smallest)
    longest = dims.index(max(dims))
    place[longest] = (place[longest] + 1) % dims[longest]
    return drawn.at[tuple(place)].set(top_value)


def levels(rng, shape, shards, low, top_value):
    level, own = 1.0, jax.random.fold_in(rng, 6)
    for dim, shards_of in shards:
        heights = jnp.exp(jax.random.uniform(jax.random.fold_in(own, dim), (shards_of,), jnp.float32, low / len(shards), top_value / len(shards)))
        level = level * jnp.repeat(heights, shape[dim] // shards_of).reshape([-1 if axis == dim else 1 for axis in range(len(shape))])
    return level


def gaussian(rng, extent, width, most, shards=(), dtype=jnp.bfloat16):
    entries = jax.random.normal(rng, extent, jnp.float32) * width
    if len(shards) > 0:
        entries = levels(rng, extent, shards, -0.22, 0.18) * entries
    return jnp.clip(entries, min=-most, max=most).astype(dtype)


def setup_inputs(seed: int = 0) -> dict:
    seeds = jax.random.split(jax.random.key(seed), 14)
    air_latent_array = gaussian(seeds[0], (MEMBERS, ALAT, ALON, AW), 1.0, 6.0, ((0, 16), (1, 32)))
    air_exchange_projection = gaussian(seeds[1], (AW, LINKED_QUANTITY), AW ** -0.5, 0.3125)
    marine_latent_array = gaussian(seeds[2], (MEMBERS, OLAT, OLON, MARINE_DIMENSION), 1.0, 6.0, ((0, 16), (2, 32)))
    driver_projection_matrix = gaussian(seeds[3], (LINKED_QUANTITY, MARINE_DIMENSION), LINKED_QUANTITY ** -0.5, 0.5)
    spatial_kernel_taps = gaussian(seeds[4], (KS * KS, MARINE_DIMENSION), 0.33, 1.5, (), jnp.float32)
    layernorm_multiplier = jnp.clip(1.0 + 0.15 * jax.random.normal(seeds[5], (MARINE_DIMENSION,), jnp.float32), 0.25, 1.75)
    pointwise_widen_matrix = gaussian(seeds[6], (MARINE_DIMENSION, HID), MARINE_DIMENSION ** -0.5, 0.375)
    pointwise_shrink_matrix = gaussian(seeds[7], (HID, MARINE_DIMENSION), HID ** -0.5, 0.1875)
    thermal_projection_matrix = gaussian(seeds[8], (MARINE_DIMENSION, LINKED_QUANTITY), MARINE_DIMENSION ** -0.5, 0.375)
    intersecting_air_sites = draw_intersecting_air_sites(jax.random.fold_in(seeds[13], 71), 0)
    margin_multiplier = plant(jax.random.randint(seeds[10], (K, OLAT, OLON), 1, 9), jax.random.fold_in(seeds[10], 1), 1, 8).astype(jnp.int32)
    terrain_water_indicator = draw_terrain_water_indicator(jax.random.fold_in(seeds[13], 71), 0)
    marine_successor_adjoint = gaussian(seeds[12], (MEMBERS, OLAT, OLON, MARINE_DIMENSION), 1.0, 6.0, ((0, 16), (2, 32)))
    return {"air_latent_array": air_latent_array, "air_exchange_projection": air_exchange_projection, "marine_latent_array": marine_latent_array, "driver_projection_matrix": driver_projection_matrix, "spatial_kernel_taps": spatial_kernel_taps, "layernorm_multiplier": layernorm_multiplier, "pointwise_widen_matrix": pointwise_widen_matrix, "pointwise_shrink_matrix": pointwise_shrink_matrix, "thermal_projection_matrix": thermal_projection_matrix, "intersecting_air_sites": intersecting_air_sites, "margin_multiplier": margin_multiplier, "terrain_water_indicator": terrain_water_indicator, "marine_successor_adjoint": marine_successor_adjoint}


def layer_norm(values, gain):
    centred = values - lax.optimization_barrier(jnp.mean(values, axis=-1, keepdims=True))
    spread = lax.optimization_barrier(jnp.mean(centred * centred, axis=-1, keepdims=True))
    return centred * lax.rsqrt(spread + 1e-06) * gain

def regrid(flat_fluxes, cell_ids, margin):
    picked = jnp.take(flat_fluxes, cell_ids, axis=0).astype(jnp.float32)
    factor = margin.astype(jnp.float32)
    weighted = lax.optimization_barrier(jnp.sum(factor[..., None] * picked, axis=0))
    return (weighted / lax.optimization_barrier(jnp.sum(factor, axis=0))[..., None]).astype(jnp.bfloat16)

def marine_update_kernel(marine_present_latent, marine_driver_input, latent_adjoint, water_indicator_real, driver_projection_matrix, spatial_kernel_taps, layernorm_multiplier, pointwise_widen_matrix, pointwise_shrink_matrix, thermal_projection_matrix, haloed_latent, haloed_derivative):
    horizontal_sum_result, vertical_sum_result, feature_dimension = marine_present_latent.shape
    reach = KS // 2
    forcing_flat = marine_driver_input.reshape(-1, marine_driver_input.shape[-1])
    pushed = jnp.dot(forcing_flat, driver_projection_matrix, preferred_element_type=jnp.float32).reshape(horizontal_sum_result, vertical_sum_result, feature_dimension)
    mixed = (marine_present_latent.astype(jnp.float32) + pushed).astype(jnp.bfloat16)
    padded = jnp.pad(haloed_latent(mixed), ((reach, reach), (0, 0), (0, 0))).astype(jnp.float32)
    conv_out = jnp.zeros((horizontal_sum_result, vertical_sum_result, feature_dimension), jnp.float32)
    for row_off in range(KS):
        for col_off in range(KS):
            conv_out = conv_out + spatial_kernel_taps[row_off * KS + col_off] * padded[row_off:row_off + horizontal_sum_result, col_off:col_off + vertical_sum_result]
    normed_f, pull_norm = jax.vjp(layer_norm, conv_out.reshape(-1, feature_dimension), layernorm_multiplier)
    normed = normed_f.astype(jnp.bfloat16)
    hidden_pre = jnp.dot(normed, pointwise_widen_matrix, preferred_element_type=jnp.float32)
    hidden_f, pull_gelu = jax.vjp(jax.nn.gelu, hidden_pre)
    hidden = hidden_f.astype(jnp.bfloat16)
    mlp_out = jnp.dot(hidden, pointwise_shrink_matrix, preferred_element_type=jnp.float32)
    sea_column = water_indicator_real.reshape(-1, 1)
    marine_successor_latent = (sea_column * (mixed.reshape(-1, feature_dimension).astype(jnp.float32) + mlp_out)).astype(jnp.bfloat16)
    thermal_highres_field = jnp.dot(marine_successor_latent, thermal_projection_matrix, preferred_element_type=jnp.float32)
    thermal_highres_field = thermal_highres_field.reshape(horizontal_sum_result // SUBDIVISION, SUBDIVISION, vertical_sum_result // SUBDIVISION, SUBDIVISION, thermal_highres_field.shape[-1])
    marine_site_number = lax.optimization_barrier(jnp.sum(water_indicator_real.reshape(horizontal_sum_result // SUBDIVISION, SUBDIVISION, vertical_sum_result // SUBDIVISION, SUBDIVISION), axis=(1, 3)))
    thermal_lowres_field = (lax.optimization_barrier(jnp.sum(thermal_highres_field, axis=(1, 3))) / jnp.maximum(marine_site_number, 1.0)[..., None]).astype(jnp.bfloat16)
    masked_cot = (sea_column * latent_adjoint.reshape(-1, feature_dimension).astype(jnp.float32)).astype(jnp.bfloat16)
    grad_down = jnp.dot(hidden.T, masked_cot, preferred_element_type=jnp.float32)
    hidden_cot = jnp.dot(masked_cot, pointwise_shrink_matrix.T, preferred_element_type=jnp.float32)
    pre_cot = pull_gelu(hidden_cot)[0].astype(jnp.bfloat16)
    grad_up = jnp.dot(normed.T, pre_cot, preferred_element_type=jnp.float32)
    normed_cot = jnp.dot(pre_cot, pointwise_widen_matrix.T, preferred_element_type=jnp.float32)
    conv_cot, grad_gain = pull_norm(normed_cot)
    conv_cot = conv_cot.reshape(horizontal_sum_result, vertical_sum_result, feature_dimension)
    tap_grads = []
    for row_off in range(KS):
        for col_off in range(KS):
            tap_grads.append(lax.optimization_barrier(jnp.sum(conv_cot * padded[row_off:row_off + horizontal_sum_result, col_off:col_off + vertical_sum_result], axis=(0, 1))))
    grad_padded = jnp.pad(haloed_derivative(conv_cot), ((reach, reach), (0, 0), (0, 0)))
    back = masked_cot.astype(jnp.float32).reshape(horizontal_sum_result, vertical_sum_result, feature_dimension)
    for row_off in range(KS):
        for col_off in range(KS):
            row_from = KS - 1 - row_off
            col_from = KS - 1 - col_off
            back = back + spatial_kernel_taps[row_off * KS + col_off] * grad_padded[row_from:row_from + horizontal_sum_result, col_from:col_from + vertical_sum_result]
    marine_latent_adjoint = back.astype(jnp.bfloat16)
    grad_force = jnp.dot(forcing_flat.T, marine_latent_adjoint.reshape(-1, feature_dimension), preferred_element_type=jnp.float32)
    derivative_sequence = (grad_force, jnp.stack(tap_grads), grad_gain, grad_up, grad_down)
    return (marine_successor_latent.reshape(horizontal_sum_result, vertical_sum_result, feature_dimension), thermal_lowres_field, marine_latent_adjoint, derivative_sequence)

def periodic_extended_lanes(values):
    reach = KS // 2
    return jnp.concatenate([values[:, -reach:], values, values[:, :reach]], axis=1)

def reference(air_latent_array, air_exchange_projection, marine_latent_array, driver_projection_matrix, spatial_kernel_taps, layernorm_multiplier, pointwise_widen_matrix, pointwise_shrink_matrix, thermal_projection_matrix, intersecting_air_sites, margin_multiplier, terrain_water_indicator, marine_successor_adjoint):
    strip_of = (jnp.arange(OLON) // OCOLS).astype(jnp.int32)
    global_ids = (intersecting_air_sites // ACOLS * ALON + strip_of[None, None, :] * ACOLS + intersecting_air_sites % ACOLS).astype(jnp.int32)
    water_indicator_real = terrain_water_indicator.astype(jnp.float32)

    def sample_replica(member_args):
        atmos, marine_present_latent, latent_adjoint = member_args
        fluxes = jnp.dot(atmos.reshape(-1, AW), air_exchange_projection, preferred_element_type=jnp.float32).astype(jnp.bfloat16)
        marine_driver_input = regrid(fluxes, global_ids, margin_multiplier)
        return marine_update_kernel(marine_present_latent, marine_driver_input, latent_adjoint, water_indicator_real, driver_projection_matrix, spatial_kernel_taps, layernorm_multiplier, pointwise_widen_matrix, pointwise_shrink_matrix, thermal_projection_matrix, periodic_extended_lanes, periodic_extended_lanes)
    successor_latent_tensor, thermal_tensor, derivative_tensor, derivative_sequence = lax.map(sample_replica, (air_latent_array, marine_latent_array, marine_successor_adjoint))
    grad_scale = 1.0 / math.sqrt(MEMBERS * OLAT * OLON)
    accumulated_result = [(lax.optimization_barrier(jnp.sum(values, axis=0)) * grad_scale).astype(jnp.bfloat16) for values in derivative_sequence]
    return (successor_latent_tensor, thermal_tensor, derivative_tensor, accumulated_result[0], accumulated_result[1], accumulated_result[2], accumulated_result[3], accumulated_result[4])
```

```python
import functools
import math

import jax
import jax.numpy as jnp
from jax import lax
from jax.experimental import pallas as pl
from jax.experimental.pallas import tpu as pltpu
from jax.sharding import Mesh
from jax.sharding import PartitionSpec as P

F32 = jnp.float32
BF16 = jnp.bfloat16
ENS = ("ens_0", "ens_1")
TILE = ("tile_0", "tile_1")
Z, CORE = TILE

ROWS = 128
OWN = 8
CH = 256
HID = 1024
LINK = 128
MARGINS = 4
WIDE = OWN + 4
MID = OWN + 2
HALO = 3 * ROWS + 16
XY = 16
ZS = 16
BIG = 128
CHUNK = 152
PIECE = 16
GELU_A = math.sqrt(2.0 / math.pi)
GELU_B = GELU_A * 0.044715


def call(kernel, out_shape, scratch=(), limit=24, flops=0, moved=0, smem=(), far=()):
    def run(*args):
        args = [
            pltpu.with_memory_space_constraint(arg, pltpu.HBM) if i in far else arg
            for i, arg in enumerate(args)
        ]

        def space(i):
            if i in smem:
                return pltpu.SMEM
            return pltpu.HBM if i in far else pltpu.VMEM

        return pl.pallas_call(
            kernel,
            out_shape=out_shape,
            in_specs=[pl.BlockSpec(memory_space=space(i)) for i in range(len(args))],
            out_specs=jax.tree.map(lambda _: pl.BlockSpec(memory_space=pltpu.VMEM), out_shape),
            scratch_shapes=list(scratch),
            compiler_params=pltpu.CompilerParams(vmem_limit_bytes=limit * 2**20),
            cost_estimate=pl.CostEstimate(flops=flops, bytes_accessed=moved, transcendentals=0),
        )(*args)

    return run


def shape(*dims, dtype=BF16):
    return jax.ShapeDtypeStruct(dims, dtype)


def held(*dims, dtype=BF16):
    return pltpu.VMEM(dims, dtype)


def dot(a, b, contract=((1,), (0,))):
    return lax.dot_general(a, b, (contract, ((), ())), preferred_element_type=F32)


NT = ((1,), (1,))
TN = ((0,), (0,))


CELLS = ROWS * OWN


def put_rows(turned, value):
    flat = value.astype(F32).reshape(CELLS, CH)
    turned[pl.ds(0, CELLS), :] = flat[:, :128]
    turned[pl.ds(CELLS, CELLS), :] = flat[:, 128:]


def column(turned, c):
    low = turned[pl.ds(c, ROWS, stride=OWN), :]
    high = turned[pl.ds(CELLS + c, ROWS, stride=OWN), :]
    return jnp.concatenate([low, high], axis=1)


def put_column(turned, c, value):
    turned[pl.ds(c, ROWS, stride=OWN), :] = value[:, :128]
    turned[pl.ds(CELLS + c, ROWS, stride=OWN), :] = value[:, 128:]


def rows_of(turned):
    flat = jnp.concatenate([turned[pl.ds(0, CELLS), :], turned[pl.ds(CELLS, CELLS), :]], axis=1)
    return flat.reshape(ROWS, OWN, CH).astype(BF16)


def fetch(sources, targets, sems):
    copies = [
        pltpu.make_async_copy(source, target, sems.at[i])
        for i, (source, target) in enumerate(zip(sources, targets, strict=True))
    ]
    for copy in copies:
        copy.start()
    return copies


def sea_columns(water):
    eye = lax.broadcasted_iota(jnp.int32, (ROWS, ROWS), 0) == lax.broadcasted_iota(
        jnp.int32, (ROWS, ROWS), 1
    )
    ones = jnp.ones((ROWS, CH), BF16)
    wet = water[...].astype(F32)

    def one(c):
        spread = jnp.where(eye, jnp.broadcast_to(wet[c : c + 1], (ROWS, ROWS)), 0.0)
        return dot(spread.astype(BF16), ones)

    return one


def start_kernel(
    air_far,
    head_far,
    lat_far,
    adj_far,
    water_far,
    sites_far,
    margin_far,
    out,
    to_left,
    to_right,
    air,
    head,
    lat,
    adj,
    water,
    sites,
    margin,
    sems,
    wrapped,
    turned,
):
    copies = fetch(
        (air_far, head_far, lat_far, adj_far, water_far, sites_far, margin_far),
        (air, head, lat, adj, water, sites, margin),
        sems,
    )
    copies[0].wait()
    copies[1].wait()
    fluxes = dot(air[...], head[...])
    wrapped[pl.ds(8, 64), :] = fluxes
    wrapped[pl.ds(0, 8), :] = fluxes[56:64]
    wrapped[pl.ds(72, 8), :] = fluxes[0:8]
    for tile in range(32):
        out[tile] = wrapped[pl.ds(6 + 2 * tile, 8), :].astype(BF16)
    copies[2].wait()
    sides = ((to_left, 0, 0), (to_right, OWN - 2, OWN - 1))
    put_rows(turned, lat[...])
    for ref, first, edge in sides:
        for q in range(2):
            ref[pl.ds(q * ROWS, ROWS), :] = column(turned, first + q).astype(BF16)
    copies[3].wait()
    copies[4].wait()
    put_rows(turned, adj[...])
    sea = sea_columns(water)
    for ref, first, edge in sides:
        ref[pl.ds(2 * ROWS, ROWS), :] = (column(turned, edge) * sea(edge)).astype(BF16)
    copies[5].wait()
    copies[6].wait()
    for ref, first, edge in sides:
        ids = jnp.concatenate([sites[k, first : first + 2, :] for k in range(MARGINS)], axis=0)
        weights = jnp.concatenate([margin[k, first : first + 2, :] for k in range(MARGINS)], axis=0)
        packed = jnp.concatenate([ids, weights], axis=1).astype(F32)
        ref[pl.ds(3 * ROWS, 16), :] = jnp.concatenate(
            [packed, jnp.zeros_like(packed)], axis=0
        ).astype(BF16)


def own_kernel(
    lat_far, adj_far, water, lat_out, cot_out, cot_t, sea_out, inverse, lat, adj, sems, turned, sums
):
    copies = fetch((lat_far, adj_far), (lat, adj), sems)
    sea = sea_columns(water)
    masks = [sea(c) for c in range(OWN)]
    for c in range(OWN):
        sea_out[pl.ds(c * ROWS, ROWS), :] = masks[c][:, :LINK].astype(BF16)
    for half in range(2):
        sums[...] = sum(masks[half * 4 + c][:, :LINK] for c in range(4))
        for side in range(2):
            count = sum(sums[pl.ds(4 * side + i, ZS, stride=8), :] for i in range(4))
            inverse[2 * half + side] = 1.0 / jnp.maximum(count, 1.0)
    copies[0].wait()
    put_rows(turned, lat[...])
    for c in range(OWN):
        lat_out[pl.ds(c * ROWS, ROWS), :] = column(turned, c).astype(BF16)
    copies[1].wait()
    put_rows(turned, adj[...])
    for c in range(OWN):
        cot = column(turned, c) * masks[c]
        cot_out[pl.ds(c * ROWS, ROWS), :] = cot.astype(BF16)
        cot_t[:, pl.ds(c * ROWS, ROWS)] = jnp.transpose(cot).astype(BF16)


def weight_kernel(sites, margin, left, right, out):
    place = lax.broadcasted_iota(jnp.int32, (256, ROWS), 0)
    edges = [ref[pl.ds(3 * ROWS, 16), :].astype(F32) for ref in (left, right)]
    for e in range(WIDE):
        total = jnp.zeros((256, ROWS), F32)
        for k in range(MARGINS):
            if 2 <= e < 2 + OWN:
                ids = sites[k, e - 2 : e - 1, :]
                weight = margin[k, e - 2 : e - 1, :].astype(F32)
                shift = 2
            else:
                side, q, shift = (0, e, 0) if e < 2 else (1, e - 2 - OWN, 4)
                row = edges[side][2 * k + q : 2 * k + q + 1]
                ids = row[:, :ROWS].astype(jnp.int32)
                weight = row[:, ROWS:]
            spot = (ids >> 1) * 8 + (ids & 1) + shift
            total = total + jnp.where(place == spot, weight, 0.0)
        out[pl.ds(e * ROWS, ROWS), :] = jnp.transpose(total).astype(BF16)


PAD = ROWS + 16


def clear_pads(ref):
    zeros = jnp.zeros((8, LINK), F32)
    for i in range(ref.shape[0]):
        ref[i, pl.ds(0, 8), :] = zeros
        ref[i, pl.ds(8 + ROWS, 8), :] = zeros


def ocean_kernel(
    core,
    flux,
    weights,
    lat,
    left,
    right,
    cot,
    cot_t,
    drive_far,
    taps_far,
    gain_far,
    widen_far,
    shrink_far,
    keep,
    send,
    mixed,
    forcing,
    xhat,
    rstd,
    back,
    mlp,
    drive,
    taps,
    gain,
    widen,
    shrink,
    sems,
    normed,
    up,
    down,
):
    copies = fetch(
        (drive_far, taps_far, gain_far, widen_far, shrink_far),
        (drive, taps, gain, widen, shrink),
        sems,
    )
    clear_pads(mixed)
    source = jnp.concatenate([flux[...], jnp.ones((256, LINK), BF16)], axis=1)
    both = dot(weights[...], source)
    force = (both[:, :LINK] / both[:, LINK:]).astype(BF16)
    forcing[...] = force[2 * ROWS : 2 * ROWS + CELLS]
    for copy in copies[:3]:
        copy.wait()
    pushed = dot(force, drive[...])
    for e in range(WIDE):
        if e < 2:
            state = left[pl.ds(e * ROWS, ROWS), :]
        elif e < 2 + OWN:
            state = lat[pl.ds((e - 2) * ROWS, ROWS), :]
        else:
            state = right[pl.ds((e - 2 - OWN) * ROWS, ROWS), :]
        value = state.astype(F32) + pushed[e * ROWS : (e + 1) * ROWS]
        value = value.astype(BF16).astype(F32)
        for h in range(2):
            mixed[2 * e + h, pl.ds(8, ROWS), :] = value[:, h * LINK : (h + 1) * LINK]
    tap = taps[...]
    scale = gain[...]

    def forward(n, carry):
        convs = []
        for h in range(2):
            total = None
            for a in range(3):
                for b in range(3):
                    part = (
                        tap[3 * a + b : 3 * a + b + 1, h * LINK : (h + 1) * LINK]
                        * mixed[2 * (n + b) + h, pl.ds(7 + a, ROWS), :]
                    )
                    total = part if total is None else total + part
            convs.append(total)
        mean = jnp.sum(convs[0] + convs[1], axis=1, keepdims=True) * (1.0 / CH)
        centred = [conv - mean for conv in convs]
        squares = centred[0] * centred[0] + centred[1] * centred[1]
        inv = lax.rsqrt(jnp.sum(squares, axis=1, keepdims=True) * (1.0 / CH) + 1e-6)
        hat = jnp.concatenate([c * inv for c in centred], axis=1)
        rows = pl.ds(pl.multiple_of(n * ROWS, ROWS), ROWS)
        xhat[rows, :] = hat
        rstd[rows, :] = jnp.broadcast_to(inv, (ROWS, LINK))
        normed[rows, :] = (hat * scale).astype(BF16)
        return carry

    lax.fori_loop(0, MID, forward, 0)
    for copy in copies[3:]:
        copy.wait()
    norm = normed[...]
    norm_t = jnp.transpose(norm[ROWS : ROWS + CELLS])
    cots = jnp.concatenate(
        [left[pl.ds(2 * ROWS, ROWS), :], cot[...], right[pl.ds(2 * ROWS, ROWS), :]], axis=0
    )
    for j in range(4):
        cols = pl.ds(j * 256, 256)
        pre = dot(norm, widen[:, cols])
        square = pre * pre
        bend = jnp.tanh(pre * (GELU_A + GELU_B * square))
        half = 0.5 * pre
        more = 1.0 + bend
        hidden = (half * more).astype(BF16)[ROWS : ROWS + CELLS]
        slope = 0.5 * more + half * (1.0 - bend * bend) * (GELU_A + 3.0 * GELU_B * square)
        hidden_cot = dot(cots, shrink[cols, :], NT)
        pre_cot = (hidden_cot * slope).astype(BF16)
        up[:, cols] = dot(norm_t, pre_cot[ROWS : ROWS + CELLS])
        down[cols, :] = jnp.transpose(dot(cot_t[...], hidden))
        add_mlp = dot(hidden, shrink[cols, :])
        add_back = dot(pre_cot, widen[:, cols], NT)
        if j == 0:
            mlp[...] = add_mlp
            back[...] = add_back
        else:
            mlp[...] += add_mlp
            back[...] += add_back

    for which, out in ((0, keep), (1, send)):
        side = core[0] if which == 0 else 1 - core[0]
        for xy in range(XY):
            rows_up = up[pl.ds(pl.multiple_of(side * 128 + xy * 8, 8), 8), :]
            rows_down = down[pl.ds(pl.multiple_of(side * 512 + xy * 32, 32), 32), :]
            tiles = [rows_up[:, z * 128 : (z + 1) * 128] for z in range(8)]
            for g in range(4):
                for lane in range(2):
                    tiles.append(rows_down[g * 8 : g * 8 + 8, lane * 128 : lane * 128 + 128])
            out[xy] = jnp.concatenate(tiles, axis=0).astype(out.dtype)


def rest_kernel(
    mixed,
    forcing,
    xhat,
    rstd,
    back,
    mlp,
    cot,
    sea,
    inverse,
    core,
    taps_far,
    gain_far,
    thermal_far,
    succ_out,
    sst_near,
    sst_across,
    adj_out,
    small,
    taps,
    gain,
    thermal,
    sems,
    curve,
    turned,
    sums,
):
    copies = fetch(
        (gain_far, taps_far, thermal_far), (gain, taps, thermal),
        sems,
    )
    clear_pads(curve)
    for copy in copies[:2]:
        copy.wait()
    scale = gain[...]
    tap = taps[...]

    def backward(n, total):
        rows = pl.ds(pl.multiple_of(n * ROWS, ROWS), ROWS)
        normed_cot = back[rows, :]
        hat = xhat[rows, :]
        grown = normed_cot * scale
        mean = jnp.mean(grown, axis=1, keepdims=True)
        along = jnp.mean(grown * hat, axis=1, keepdims=True)
        inv = rstd[rows, :]
        for h in range(2):
            part = slice(h * LINK, (h + 1) * LINK)
            curve[2 * n + h, pl.ds(8, ROWS), :] = inv * (grown[:, part] - mean - hat[:, part] * along)
        inside = jnp.logical_and(n >= 1, n <= OWN)
        product = jnp.sum((normed_cot * hat).reshape(ROWS // 8, 8, CH), axis=0)
        return total + jnp.where(inside, product, 0.0)

    gain_sum = lax.fori_loop(0, MID, backward, jnp.zeros((8, CH), F32))
    gain_grad = jnp.sum(gain_sum, axis=0, keepdims=True)
    for copy in copies[2:]:
        copy.wait()

    def eightfold(x):
        return jnp.sum(x.reshape(ROWS // 8, 8, LINK), axis=0)

    tap_grads = [[jnp.zeros((8, LINK), F32) for _ in range(9)] for _ in range(2)]
    for c in range(OWN):
        halves = []
        for h in range(2):
            lanes = slice(h * LINK, (h + 1) * LINK)
            moved = [curve[2 * (c + 1) + h, pl.ds(9 - a, ROWS), :] for a in range(3)]
            around = [mixed[2 * (c + 1 + b) + h, pl.ds(8, ROWS), :] for b in range(3)]
            for a in range(3):
                for b in range(3):
                    tap_grads[h][3 * a + b] += eightfold(moved[a] * around[b])
            total = cot[pl.ds(c * ROWS, ROWS), lanes].astype(F32)
            for b in range(3):
                for a in range(3):
                    near = moved[a] if b == 1 else curve[2 * (c + 2 - b) + h, pl.ds(9 - a, ROWS), :]
                    total = total + tap[3 * a + b : 3 * a + b + 1, lanes] * near
            halves.append(total)
        value = jnp.concatenate(halves, axis=1).astype(BF16)
        put_column(turned, c, value.astype(F32))
        part = dot(forcing[pl.ds(c * ROWS, ROWS), :], value, TN)
        force_grad = part if c == 0 else force_grad + part
    adj_out[...] = rows_of(turned)

    rest = jnp.concatenate(
        [
            jnp.concatenate(
                [jnp.sum(tap_grads[h][t], axis=0, keepdims=True) for h in range(2)], axis=1
            )
            for t in range(9)
        ]
        + [gain_grad],
        axis=0,
    )
    for xy in range(XY):
        rows = force_grad[xy * 8 : xy * 8 + 8]
        tail = jnp.zeros((8, LINK), F32)
        if xy < 10:
            row = rest[xy : xy + 1]
            tail = jnp.concatenate([row[:, :128], row[:, 128:], jnp.zeros((6, LINK), F32)], axis=0)
        small[xy] = jnp.concatenate([rows[:, :128], rows[:, 128:], tail], axis=0)

    fine = [None, None]
    for c in range(OWN):
        mask = sea[pl.ds(c * ROWS, ROWS), :].astype(F32)
        state = [
            mask * (mixed[2 * (c + 2) + h, pl.ds(8, ROWS), :] + mlp[pl.ds(c * ROWS, ROWS), h * LINK : (h + 1) * LINK])
            for h in range(2)
        ]
        value = jnp.concatenate(state, axis=1).astype(BF16)
        put_column(turned, c, value.astype(F32))
        part = dot(value, thermal[...])
        fine[c // 4] = part if c % 4 == 0 else fine[c // 4] + part
    succ_out[...] = rows_of(turned)
    for half in range(2):
        sums[...] = fine[half]
        for side, out in ((core[0], sst_near), (1 - core[0], sst_across)):
            coarse = sum(sums[pl.ds(4 * side + i, ZS, stride=8), :] for i in range(4))
            out[half] = (coarse * inverse[2 * half + side]).astype(BF16)


def core_sum_kernel(keep, got, small, out):
    for xy in range(XY):
        out[xy, pl.ds(0, BIG), :] = (keep[xy] + got[xy].astype(F32)).astype(BF16)
        rest = small[xy]
        out[xy, pl.ds(BIG, 16), :] = rest[:16].astype(BF16)
        out[xy, pl.ds(BIG + 16, 8), :] = rest[16:].astype(BF16)


def xy_sum_kernel(got, near, across, out):
    total = got[0].astype(F32)
    for xy in range(1, XY):
        total = total + got[xy].astype(F32)
    row = lax.broadcasted_iota(jnp.int32, (8, LINK), 0)
    surface = [ref[half].astype(F32) for ref in (near, across) for half in range(2)]
    for z in range(ZS):
        rows = [total[BIG + z : BIG + z + 1]]
        rows.append(total[BIG + 16 + z : BIG + 17 + z] if z < 2 else jnp.zeros((1, LINK), F32))
        rows += [values[z : z + 1] for values in surface]
        lower = jnp.zeros((8, LINK), F32)
        for i, values in enumerate(rows):
            lower = jnp.where(row == i, jnp.broadcast_to(values, (8, LINK)), lower)
        out[z] = jnp.concatenate([total[z * 8 : z * 8 + 8], lower], axis=0).astype(BF16)


def z_sum_kernel(factor, core, got, out, sst):
    total = got[0].astype(F32)
    for z in range(1, ZS):
        total = total + got[z].astype(F32)
    value = (total * factor).astype(BF16)
    for z in range(ZS):
        out[z] = value
    own_first = core[0] == 0
    blocks = []
    for z in range(ZS):
        near, across = got[z, 8:16, :].astype(F32)[2:4], got[z, 8:16, :].astype(F32)[4:6]
        blocks.append(jnp.where(own_first, near, across))
        blocks.append(jnp.where(own_first, across, near))
    sst[...] = jnp.concatenate(blocks, axis=0).astype(BF16)


def spread_kernel(got, out):
    pieces = [got[z].astype(F32) for z in range(ZS)]
    big = jnp.concatenate([p[:8] for p in pieces], axis=0)
    force = jnp.concatenate([p[8:9] for p in pieces], axis=0)
    rest = jnp.concatenate([p[9:10] for p in pieces[:8]], axis=0)
    value = jnp.concatenate([big, force, rest], axis=0).astype(BF16)
    for xy in range(XY):
        out[xy] = value


def final_kernel(core, mine, other, up_out, down_out, force_out, conv_out, gain_out):
    for which, ref in ((0, mine), (1, other)):
        side = core[0] if which == 0 else 1 - core[0]
        ups, downs = [], []
        for xy in range(XY):
            block = ref[xy, pl.ds(0, BIG), :].astype(F32)
            tiles = [block[z * 8 : z * 8 + 8] for z in range(ZS)]
            ups.append(jnp.concatenate(tiles[:8], axis=1))
            for g in range(4):
                downs.append(jnp.concatenate(tiles[8 + 2 * g : 10 + 2 * g], axis=1))
        up_out[pl.ds(pl.multiple_of(side * 128, 128), 128), :] = jnp.concatenate(
            ups, axis=0
        ).astype(BF16)
        down_out[pl.ds(pl.multiple_of(side * 512, 512), 512), :] = jnp.concatenate(
            downs, axis=0
        ).astype(BF16)
    rows, rest = [], []
    for xy in range(XY):
        tail = mine[xy, pl.ds(BIG, 24), :].astype(F32) + other[xy, pl.ds(BIG, 24), :].astype(F32)
        rows.append(jnp.concatenate([tail[:8], tail[8:16]], axis=1))
        if xy < 10:
            rest.append(jnp.concatenate([tail[16:17], tail[17:18]], axis=1))
    force_out[...] = jnp.concatenate(rows, axis=0).astype(BF16)
    conv_out[...] = jnp.concatenate(rest[:9], axis=0).astype(BF16)
    gain_out[...] = rest[9].astype(BF16)


def body(
    air,
    head,
    lat,
    drive,
    taps,
    gain,
    widen,
    shrink,
    thermal,
    sites,
    margin,
    water,
    adj,
):
    core = lax.axis_index(CORE).astype(jnp.int32).reshape(1)
    sites_t = jnp.transpose(sites, (0, 2, 1))
    margin_t = jnp.transpose(margin, (0, 2, 1))
    water_t = jnp.transpose(water)
    fluxes, to_left, to_right = call(
        start_kernel,
        (shape(32, 8, LINK), shape(HALO, CH), shape(HALO, CH)),
        [
            pltpu.VMEM((64, air.shape[-1]), BF16),
            pltpu.VMEM(head.shape, BF16),
            pltpu.VMEM((ROWS, OWN, CH), BF16),
            pltpu.VMEM((ROWS, OWN, CH), BF16),
            pltpu.VMEM((OWN, ROWS), jnp.int32),
            pltpu.VMEM((MARGINS, OWN, ROWS), jnp.int32),
            pltpu.VMEM((MARGINS, OWN, ROWS), jnp.int32),
            pltpu.SemaphoreType.DMA((7,)),
            pltpu.VMEM((80, LINK), F32),
            pltpu.VMEM((2 * CELLS, LINK), F32),
        ],
        limit=56,
        moved=2_000_000,
        far=range(7),
    )(air.reshape(64, -1), head, lat[0], adj[0], water_t, sites_t, margin_t)
    ring = [(i, (i + 1) % 32) for i in range(32)]
    left = lax.ppermute(to_right, TILE, ring)
    right = lax.ppermute(to_left, TILE, [(b, a) for a, b in ring])
    flux_in = lax.all_to_all(fluxes, TILE, 0, 0, tiled=True)
    lat_own, cot, cot_t, sea, inverse = call(
        own_kernel,
        (
            held(CELLS, CH),
            held(CELLS, CH),
            held(CH, CELLS),
            held(CELLS, LINK),
            held(4, ROWS // 8, LINK, dtype=F32),
        ),
        [
            pltpu.VMEM((ROWS, OWN, CH), BF16),
            pltpu.VMEM((ROWS, OWN, CH), BF16),
            pltpu.SemaphoreType.DMA((2,)),
            pltpu.VMEM((2 * CELLS, LINK), F32),
            pltpu.VMEM((ROWS, LINK), F32),
        ],
        moved=4_000_000,
        far=(0, 1),
    )(lat[0], adj[0], water_t)
    weights = call(weight_kernel, held(WIDE * ROWS, 256), moved=1_000_000)(
        sites_t, margin_t, left, right
    )
    gain_row = gain.reshape(1, CH)
    keep, send, mixed, forcing, xhat, rstd, back, mlp = call(
        ocean_kernel,
        (
            held(XY, BIG, LINK, dtype=F32),
            held(XY, BIG, LINK),
            held(2 * WIDE, PAD, LINK, dtype=F32),
            held(CELLS, LINK),
            held(MID * ROWS, CH, dtype=F32),
            held(MID * ROWS, LINK, dtype=F32),
            held(MID * ROWS, CH, dtype=F32),
            held(CELLS, CH, dtype=F32),
        ),
        [
            pltpu.VMEM((LINK, CH), BF16),
            pltpu.VMEM((9, CH), F32),
            pltpu.VMEM((1, CH), F32),
            pltpu.VMEM((CH, HID), BF16),
            pltpu.VMEM((HID, CH), BF16),
            pltpu.SemaphoreType.DMA((5,)),
            pltpu.VMEM((MID * ROWS, CH), BF16),
            pltpu.VMEM((CH, HID), F32),
            pltpu.VMEM((HID, CH), F32),
        ],
        limit=36,
        flops=4_000_000_000,
        moved=10_000_000,
        smem=(0,),
        far=range(8, 13),
    )(
        core,
        flux_in.reshape(256, LINK),
        weights,
        lat_own,
        left,
        right,
        cot,
        cot_t,
        drive,
        taps,
        gain_row,
        widen,
        shrink,
    )
    succ, sst_near, sst_across, adj_out, small = call(
        rest_kernel,
        (
            shape(ROWS, OWN, CH),
            held(2, ZS, LINK),
            held(2, ZS, LINK),
            shape(ROWS, OWN, CH),
            held(XY, 24, LINK, dtype=F32),
        ),
        [
            pltpu.VMEM((9, CH), F32),
            pltpu.VMEM((1, CH), F32),
            pltpu.VMEM((CH, LINK), BF16),
            pltpu.SemaphoreType.DMA((3,)),
            pltpu.VMEM((2 * MID, PAD, LINK), F32),
            pltpu.VMEM((2 * CELLS, LINK), F32),
            pltpu.VMEM((ROWS, LINK), F32),
        ],
        limit=24,
        flops=500_000_000,
        moved=8_000_000,
        smem=(9,),
        far=range(10, 13),
    )(mixed, forcing, xhat, rstd, back, mlp, cot, sea, inverse, core, taps, gain_row, thermal)

    swap = [(0, 1), (1, 0)]
    got = lax.ppermute(send, CORE, swap)
    stage = call(core_sum_kernel, held(XY, CHUNK, LINK), moved=2_000_000)(keep, got, small)
    across = lax.ppermute(sst_across, CORE, swap)
    stage = lax.all_to_all(stage, ENS, 0, 0, tiled=True)
    stage = call(xy_sum_kernel, held(ZS, PIECE, LINK), moved=700_000)(stage, sst_near, across)
    stage = lax.all_to_all(stage, Z, 0, 0, tiled=True)
    cells = lax.axis_size(ENS) * lax.axis_size(TILE) * CELLS
    stage, sst_out = call(
        functools.partial(z_sum_kernel, 1.0 / math.sqrt(cells)),
        (held(ZS, PIECE, LINK), shape(64, LINK)),
        moved=100_000,
        smem=(0,),
    )(core, stage)
    stage = lax.all_to_all(stage, Z, 0, 0, tiled=True)
    stage = call(spread_kernel, held(XY, CHUNK, LINK), moved=700_000)(stage)
    stage = lax.all_to_all(stage, ENS, 0, 0, tiled=True)
    other = lax.ppermute(stage, CORE, swap)
    grad_up, grad_down, grad_force, grad_conv, grad_gain = call(
        final_kernel,
        (
            shape(CH, HID),
            shape(HID, CH),
            shape(LINK, CH),
            shape(9, CH),
            shape(1, CH),
        ),
        moved=2_000_000,
        smem=(0,),
    )(core, stage, other)
    return (
        succ[None],
        sst_out.reshape(1, 1, 64, LINK),
        adj_out[None],
        grad_force,
        grad_conv,
        grad_gain.reshape(CH),
        grad_up,
        grad_down,
    )


def solution(mesh):
    finer = Mesh(mesh.devices.reshape(4, 4, 16, 2), (*ENS, *TILE))
    return jax.shard_map(
        body,
        mesh=finer,
        in_specs=(
            P(ENS, TILE, None, None),
            P(),
            P(ENS, None, TILE, None),
            P(),
            P(),
            P(),
            P(),
            P(),
            P(),
            P(None, None, TILE),
            P(None, None, TILE),
            P(None, TILE),
            P(ENS, None, TILE, None),
        ),
        out_specs=(
            P(ENS, None, TILE, None),
            P(ENS, TILE, None, None),
            P(ENS, None, TILE, None),
            P(),
            P(),
            P(),
            P(),
            P(),
        ),
        check_vma=False,
    )
```

```python
import functools
import math

import jax
import jax.numpy as jnp
from jax import lax
from jax.experimental import pallas as pl
from jax.experimental.pallas import tpu as pltpu
from jax.sharding import Mesh
from jax.sharding import PartitionSpec as P

F32 = jnp.float32
BF16 = jnp.bfloat16
ENS = ("ens_0", "ens_1")
TILE = ("far", "near", "core")
GROUP = (*ENS, "near")

ROWS = 128
OWN = 8
CH = 256
HID = 1024
LINK = 128
MARGINS = 4
WIDE = OWN + 4
MID = OWN + 2
HALO = 3 * ROWS + 16
CHUNKS = 32
FARS = 8
BIG = 64
CHUNK = 80
BLOCK = 64
PIECE = 96
GELU_A = math.sqrt(2.0 / math.pi)
GELU_B = GELU_A * 0.044715


def call(kernel, out_shape, scratch=(), limit=16, flops=0, moved=0, smem=(), far=()):
    def run(*args):
        args = [
            pltpu.with_memory_space_constraint(arg, pltpu.HBM) if i in far else arg
            for i, arg in enumerate(args)
        ]

        def space(i):
            if i in smem:
                return pltpu.SMEM
            return pltpu.HBM if i in far else pltpu.VMEM

        return pl.pallas_call(
            kernel,
            out_shape=out_shape,
            in_specs=[pl.BlockSpec(memory_space=space(i)) for i in range(len(args))],
            out_specs=jax.tree.map(lambda _: pl.BlockSpec(memory_space=pltpu.VMEM), out_shape),
            scratch_shapes=list(scratch),
            compiler_params=pltpu.CompilerParams(vmem_limit_bytes=limit * 2**20),
            cost_estimate=pl.CostEstimate(flops=flops, bytes_accessed=moved, transcendentals=0),
        )(*args)

    return run


def shape(*dims, dtype=BF16):
    return jax.ShapeDtypeStruct(dims, dtype)


def held(*dims, dtype=BF16):
    return pltpu.VMEM(dims, dtype)


def dot(a, b, contract=((1,), (0,))):
    return lax.dot_general(a, b, (contract, ((), ())), preferred_element_type=F32)


NT = ((1,), (1,))
TN = ((0,), (0,))


CELLS = ROWS * OWN


def put_rows(turned, value):
    flat = value.astype(F32).reshape(CELLS, CH)
    turned[pl.ds(0, CELLS), :] = flat[:, :128]
    turned[pl.ds(CELLS, CELLS), :] = flat[:, 128:]


def column(turned, c):
    low = turned[pl.ds(c, ROWS, stride=OWN), :]
    high = turned[pl.ds(CELLS + c, ROWS, stride=OWN), :]
    return jnp.concatenate([low, high], axis=1)


def put_column(turned, c, value):
    turned[pl.ds(c, ROWS, stride=OWN), :] = value[:, :128]
    turned[pl.ds(CELLS + c, ROWS, stride=OWN), :] = value[:, 128:]


def rows_of(turned):
    flat = jnp.concatenate([turned[pl.ds(0, CELLS), :], turned[pl.ds(CELLS, CELLS), :]], axis=1)
    return flat.reshape(ROWS, OWN, CH).astype(BF16)


def fetch(sources, targets, sems):
    copies = [
        pltpu.make_async_copy(source, target, sems.at[i])
        for i, (source, target) in enumerate(zip(sources, targets, strict=True))
    ]
    for copy in copies:
        copy.start()
    return copies


def sea_columns(water):
    eye = lax.broadcasted_iota(jnp.int32, (ROWS, ROWS), 0) == lax.broadcasted_iota(
        jnp.int32, (ROWS, ROWS), 1
    )
    ones = jnp.ones((ROWS, CH), BF16)
    wet = water[...].astype(F32)

    def one(c):
        spread = jnp.where(eye, jnp.broadcast_to(wet[c : c + 1], (ROWS, ROWS)), 0.0)
        return dot(spread.astype(BF16), ones)

    return one


def spots_of(ids, weight, shift):
    place = lax.broadcasted_iota(jnp.int32, (256, ROWS), 0)
    total = jnp.zeros((256, ROWS), F32)
    for k in range(MARGINS):
        spot = (ids[k] >> 1) * 8 + (ids[k] & 1) + shift
        total = total + jnp.where(place == spot, weight[k], 0.0)
    return jnp.transpose(total).astype(BF16)


def start_kernel(
    air_far,
    head_far,
    lat_far,
    adj_far,
    water_far,
    sites_far,
    margin_far,
    out,
    to_left,
    to_right,
    air,
    head,
    lat,
    adj,
    water,
    sites,
    margin,
    sems,
    wrapped,
    turned,
):
    copies = fetch(
        (air_far, head_far, lat_far, adj_far, water_far, sites_far, margin_far),
        (air, head, lat, adj, water, sites, margin),
        sems,
    )
    copies[0].wait()
    copies[1].wait()
    fluxes = dot(air[...], head[...])
    wrapped[pl.ds(8, 64), :] = fluxes
    wrapped[pl.ds(0, 8), :] = fluxes[56:64]
    wrapped[pl.ds(72, 8), :] = fluxes[0:8]
    for tile in range(32):
        out[tile] = wrapped[pl.ds(6 + 2 * tile, 8), :].astype(BF16)
    copies[2].wait()
    sides = ((to_left, 0, 0), (to_right, OWN - 2, OWN - 1))
    put_rows(turned, lat[...])
    for ref, first, edge in sides:
        for q in range(2):
            ref[pl.ds(q * ROWS, ROWS), :] = column(turned, first + q).astype(BF16)
    copies[3].wait()
    copies[4].wait()
    put_rows(turned, adj[...])
    sea = sea_columns(water)
    for ref, first, edge in sides:
        ref[pl.ds(2 * ROWS, ROWS), :] = (column(turned, edge) * sea(edge)).astype(BF16)
    copies[5].wait()
    copies[6].wait()
    for ref, first, edge in sides:
        ids = jnp.concatenate([sites[k, first : first + 2, :] for k in range(MARGINS)], axis=0)
        weights = jnp.concatenate([margin[k, first : first + 2, :] for k in range(MARGINS)], axis=0)
        packed = jnp.concatenate([ids, weights], axis=1).astype(F32)
        ref[pl.ds(3 * ROWS, 16), :] = jnp.concatenate(
            [packed, jnp.zeros_like(packed)], axis=0
        ).astype(BF16)


def own_kernel(
    lat_far,
    adj_far,
    drive_far,
    taps_far,
    gain_far,
    water_far,
    sites_far,
    margin_far,
    lat_out,
    cot_out,
    cot_t,
    sea_out,
    inverse,
    drive,
    taps,
    gain,
    spots,
    lat,
    adj,
    water,
    sites,
    margin,
    sems,
    turned,
    sums,
):
    copies = fetch(
        (sites_far, margin_far, water_far, lat_far, adj_far, drive_far, taps_far, gain_far),
        (sites, margin, water, lat, adj, drive, taps, gain),
        sems,
    )
    for copy in copies[:3]:
        copy.wait()
    for c in range(OWN):
        ids = [sites[k, c : c + 1, :] for k in range(MARGINS)]
        weight = [margin[k, c : c + 1, :].astype(F32) for k in range(MARGINS)]
        spots[pl.ds(c * ROWS, ROWS), :] = spots_of(ids, weight, 2)
    sea = sea_columns(water)
    masks = [sea(c) for c in range(OWN)]
    for c in range(OWN):
        sea_out[pl.ds(c * ROWS, ROWS), :] = masks[c][:, :LINK].astype(BF16)
    for half in range(2):
        sums[...] = sum(masks[half * 4 + c][:, :LINK] for c in range(4))
        for spot in range(4):
            count = sum(sums[pl.ds(4 * spot + i, FARS, stride=16), :] for i in range(4))
            inverse[4 * half + spot] = 1.0 / jnp.maximum(count, 1.0)
    copies[3].wait()
    put_rows(turned, lat[...])
    for c in range(OWN):
        lat_out[pl.ds(c * ROWS, ROWS), :] = column(turned, c).astype(BF16)
    copies[4].wait()
    put_rows(turned, adj[...])
    for c in range(OWN):
        cot = column(turned, c) * masks[c]
        cot_out[pl.ds(c * ROWS, ROWS), :] = cot.astype(BF16)
        cot_t[:, pl.ds(c * ROWS, ROWS)] = jnp.transpose(cot).astype(BF16)
    for copy in copies[5:]:
        copy.wait()


PAD = ROWS + 16


def clear_pads(ref):
    zeros = jnp.zeros((8, LINK), F32)
    for i in range(ref.shape[0]):
        ref[i, pl.ds(0, 8), :] = zeros
        ref[i, pl.ds(8 + ROWS, 8), :] = zeros


def ocean_kernel(
    place,
    flux,
    spots,
    lat,
    left,
    right,
    cot,
    cot_t,
    drive,
    taps,
    gain,
    widen_far,
    shrink_far,
    keep,
    send,
    mixed,
    forcing,
    xhat,
    rstd,
    hidden,
    pre_cot,
    widen,
    shrink,
    sems,
    normed,
    pres,
    cotangents,
    up,
    down,
):
    copies = fetch((widen_far, shrink_far), (widen, shrink), sems)
    clear_pads(mixed)
    outer = []
    for ref, shift in ((left, 0), (right, 4)):
        packed = ref[pl.ds(3 * ROWS, 16), :].astype(F32)
        for q in range(2):
            rows = [packed[2 * k + q : 2 * k + q + 1] for k in range(MARGINS)]
            ids = [row[:, :ROWS].astype(jnp.int32) for row in rows]
            outer.append(spots_of(ids, [row[:, ROWS:] for row in rows], shift))
    weights = jnp.concatenate([*outer[:2], spots[...], *outer[2:]], axis=0)
    source = jnp.concatenate([flux[...], jnp.ones((256, LINK), BF16)], axis=1)
    both = dot(weights, source)
    force = (both[:, :LINK] / both[:, LINK:]).astype(BF16)
    forcing[...] = force[2 * ROWS : 2 * ROWS + CELLS]
    pushed = dot(force, drive[...])
    for e in range(WIDE):
        if e < 2:
            state = left[pl.ds(e * ROWS, ROWS), :]
        elif e < 2 + OWN:
            state = lat[pl.ds((e - 2) * ROWS, ROWS), :]
        else:
            state = right[pl.ds((e - 2 - OWN) * ROWS, ROWS), :]
        value = state.astype(F32) + pushed[e * ROWS : (e + 1) * ROWS]
        value = value.astype(BF16).astype(F32)
        for h in range(2):
            mixed[2 * e + h, pl.ds(8, ROWS), :] = value[:, h * LINK : (h + 1) * LINK]
    tap = taps[...]
    scale = gain[...]

    def forward(n, carry):
        convs = []
        for h in range(2):
            total = None
            for a in range(3):
                for b in range(3):
                    part = (
                        tap[3 * a + b : 3 * a + b + 1, h * LINK : (h + 1) * LINK]
                        * mixed[2 * (n + b) + h, pl.ds(7 + a, ROWS), :]
                    )
                    total = part if total is None else total + part
            convs.append(total)
        mean = jnp.sum(convs[0] + convs[1], axis=1, keepdims=True) * (1.0 / CH)
        centred = [conv - mean for conv in convs]
        squares = centred[0] * centred[0] + centred[1] * centred[1]
        inv = lax.rsqrt(jnp.sum(squares, axis=1, keepdims=True) * (1.0 / CH) + 1e-6)
        hat = jnp.concatenate([c * inv for c in centred], axis=1)
        rows = pl.ds(pl.multiple_of(n * ROWS, ROWS), ROWS)
        xhat[rows, :] = hat
        rstd[rows, :] = jnp.broadcast_to(inv, (ROWS, LINK))
        normed[rows, :] = (hat * scale).astype(BF16)
        return carry

    lax.fori_loop(0, MID, forward, 0, unroll=MID)
    for copy in copies:
        copy.wait()
    norm = normed[...]
    norm_t = jnp.transpose(norm[ROWS : ROWS + CELLS])
    cots = jnp.concatenate(
        [left[pl.ds(2 * ROWS, ROWS), :], cot[...], right[pl.ds(2 * ROWS, ROWS), :]], axis=0
    )
    for j in range(4):
        cols = pl.ds(j * 256, 256)
        pres[j % 2] = dot(norm, widen[:, cols])
        cotangents[j % 2] = dot(cots, shrink[cols, :], NT)
        for first in range(0, MID * ROWS, BLOCK):
            rows = pl.ds(first, BLOCK)
            pre = pres[j % 2, rows, :]
            square = pre * pre
            bend = jnp.tanh(pre * (GELU_A + GELU_B * square))
            half = 0.5 * pre
            more = 1.0 + bend
            if ROWS <= first < ROWS + CELLS:
                hidden[pl.ds(first - ROWS, BLOCK), cols] = (half * more).astype(BF16)
            slope = 0.5 * more + half * (1.0 - bend * bend) * (GELU_A + 3.0 * GELU_B * square)
            pre_cot[rows, cols] = (cotangents[j % 2, rows, :] * slope).astype(BF16)
        up[:, cols] = dot(norm_t, pre_cot[pl.ds(ROWS, CELLS), cols])
        down[cols, :] = jnp.transpose(dot(cot_t[...], hidden[:, cols]))

    def pack(side, out):
        for g in range(CHUNKS):
            rows_up = pl.ds(side * 128 + g // 4 * 16, 16)
            rows_down = pl.ds(side * 512 + g * 16, 16)
            first = g % 4 * 256
            tiles = [up[rows_up, first : first + 128], up[rows_up, first + 128 : first + 256]]
            tiles += [down[rows_down, :128], down[rows_down, 128:]]
            out[g] = jnp.concatenate(tiles, axis=0).astype(out.dtype)

    for side in range(2):

        @pl.when(place[0] == side)
        def _():
            pack(side, keep)
            pack(1 - side, send)


def rest_kernel(
    mixed,
    forcing,
    xhat,
    rstd,
    pre_cot,
    cot,
    taps,
    gain,
    widen,
    hidden,
    shrink,
    sea,
    adj_out,
    succ_out,
    small,
    curve,
    back,
):
    clear_pads(curve)
    back[...] = dot(pre_cot[...], widen[...], NT)
    scale = gain[...]
    tap = taps[...]

    def backward(n, total):
        rows = pl.ds(pl.multiple_of(n * ROWS, ROWS), ROWS)
        normed_cot = back[rows, :]
        hat = xhat[rows, :]
        grown = normed_cot * scale
        mean = jnp.mean(grown, axis=1, keepdims=True)
        along = jnp.mean(grown * hat, axis=1, keepdims=True)
        inv = rstd[rows, :]
        for h in range(2):
            part = slice(h * LINK, (h + 1) * LINK)
            curve[2 * n + h, pl.ds(8, ROWS), :] = inv * (grown[:, part] - mean - hat[:, part] * along)
        inside = jnp.logical_and(n >= 1, n <= OWN)
        product = jnp.sum((normed_cot * hat).reshape(ROWS // 8, 8, CH), axis=0)
        return total + jnp.where(inside, product, 0.0)

    gain_sum = lax.fori_loop(
        0, MID, backward, jnp.zeros((8, CH), F32), unroll=MID
    )
    gain_grad = jnp.sum(gain_sum, axis=0, keepdims=True)

    def eightfold(x):
        return jnp.sum(x.reshape(ROWS // 8, 8, LINK), axis=0)

    tap_grads = [[jnp.zeros((8, LINK), F32) for _ in range(9)] for _ in range(2)]
    for c in range(OWN):
        halves = []
        for h in range(2):
            lanes = slice(h * LINK, (h + 1) * LINK)
            moved = [curve[2 * (c + 1) + h, pl.ds(9 - a, ROWS), :] for a in range(3)]
            around = [mixed[2 * (c + 1 + b) + h, pl.ds(8, ROWS), :] for b in range(3)]
            for a in range(3):
                for b in range(3):
                    tap_grads[h][3 * a + b] += eightfold(moved[a] * around[b])
            total = cot[pl.ds(c * ROWS, ROWS), lanes].astype(F32)
            for b in range(3):
                for a in range(3):
                    near = moved[a] if b == 1 else curve[2 * (c + 2 - b) + h, pl.ds(9 - a, ROWS), :]
                    total = total + tap[3 * a + b : 3 * a + b + 1, lanes] * near
            halves.append(total)
        value = jnp.concatenate(halves, axis=1).astype(BF16)
        adj_out[pl.ds(c * ROWS, ROWS), :] = value
    force_grad = dot(forcing[...], adj_out[...], TN)

    rest = jnp.concatenate(
        [
            jnp.concatenate(
                [jnp.sum(tap_grads[h][t], axis=0, keepdims=True) for h in range(2)], axis=1
            )
            for t in range(9)
        ]
        + [gain_grad],
        axis=0,
    )
    for g in range(CHUNKS):
        lanes = slice(g % 2 * 128, g % 2 * 128 + 128)
        tail = jnp.zeros((8, LINK), F32)
        if g < 20:
            tail = jnp.concatenate([rest[g // 2 : g // 2 + 1, lanes], tail[1:]], axis=0)
        small[g] = jnp.concatenate([force_grad[g // 2 * 8 : g // 2 * 8 + 8, lanes], tail], axis=0)
    mlp = dot(hidden[...], shrink[...])
    for c in range(OWN):
        mask = sea[pl.ds(c * ROWS, ROWS), :].astype(F32)
        for h in range(2):
            lanes = slice(h * LINK, (h + 1) * LINK)
            state = mixed[2 * (c + 2) + h, pl.ds(8, ROWS), :] + mlp[c * ROWS : (c + 1) * ROWS, lanes]
            succ_out[pl.ds(c * ROWS, ROWS), lanes] = (mask * state).astype(BF16)


def state_kernel(
    succ,
    inverse,
    adj,
    place,
    thermal_far,
    succ_out,
    sst_near,
    sst_across,
    adj_out,
    thermal,
    sem,
    turned,
    sums,
):
    wait_for = pltpu.make_async_copy(thermal_far, thermal, sem)
    wait_for.start()
    wait_for.wait()
    fine = [None, None]
    for c in range(OWN):
        value = succ[pl.ds(c * ROWS, ROWS), :]
        put_column(turned, c, value.astype(F32))
        part = dot(value, thermal[...])
        fine[c // 4] = part if c % 4 == 0 else fine[c // 4] + part
    succ_out[...] = rows_of(turned)
    for half in range(2):
        sums[...] = fine[half]
        for across, out in enumerate((sst_near, sst_across)):
            for other in range(2):
                core = jnp.bitwise_xor(place[0], across)
                spot = 2 * jnp.bitwise_xor(place[1], other) + core
                coarse = sum(sums[pl.ds(4 * spot + i, FARS, stride=16), :] for i in range(4))
                out[other, half] = (coarse * inverse[4 * half + spot]).astype(BF16)
    for c in range(OWN):
        put_column(turned, c, adj[pl.ds(c * ROWS, ROWS), :].astype(F32))
    adj_out[...] = rows_of(turned)


def core_sum_kernel(keep, got, small, out):
    for g in range(CHUNKS):
        out[g, pl.ds(0, BIG), :] = (keep[g] + got[g].astype(F32)).astype(BF16)
        out[g, pl.ds(BIG, 16), :] = small[g].astype(BF16)


def group_sum_kernel(got, near, across, out):
    total = got[0].astype(F32)
    for g in range(1, CHUNKS):
        total = total + got[g].astype(F32)
    value = total.astype(BF16)
    row = lax.broadcasted_iota(jnp.int32, (8, LINK), 0)
    surface = [ref[i, half].astype(F32) for i in range(2) for ref in (near, across) for half in range(2)]
    for far in range(FARS):
        lower = jnp.broadcast_to(surface[0][far : far + 1], (8, LINK))
        for i in range(1, 8):
            lower = jnp.where(row == i, jnp.broadcast_to(surface[i][far : far + 1], (8, LINK)), lower)
        out[far, pl.ds(0, CHUNK), :] = value
        out[far, pl.ds(CHUNK, 16), :] = jnp.concatenate([lower, lower], axis=0).astype(BF16)


def far_sum_kernel(factor, got, out, surface):
    total = got[0, pl.ds(0, CHUNK), :].astype(F32)
    for far in range(1, FARS):
        total = total + got[far, pl.ds(0, CHUNK), :].astype(F32)
    value = (total * factor).astype(BF16)
    for g in range(CHUNKS):
        out[g] = value
    for far in range(FARS):
        surface[far] = got[far, pl.ds(CHUNK, 16), :]


def final_kernel(place, mine, other, kept, moved, up_out, down_out, force_out, conv_out, gain_out, sst):
    def unpack(side, ref):
        for row in range(8):
            tiles = [ref[4 * row + i, pl.ds(t * 16, 16), :] for i in range(4) for t in range(2)]
            up_out[pl.ds(side * 128 + row * 16, 16), :] = jnp.concatenate(tiles, axis=1)
        for g in range(CHUNKS):
            tiles = [ref[g, pl.ds(32 + t * 16, 16), :] for t in range(2)]
            down_out[pl.ds(side * 512 + g * 16, 16), :] = jnp.concatenate(tiles, axis=1)

    for side in range(2):

        @pl.when(place[0] == side)
        def _():
            unpack(side, mine)
            unpack(1 - side, other)

    blocks = []
    for far in range(FARS):
        own, came = kept[far].astype(F32)[0:4], moved[far].astype(F32)[4:8]
        pairs = []
        for part in (own, came):
            swapped = jnp.concatenate([part[2:4], part[0:2]], axis=0)
            pairs.append(jnp.where(place[0] == 0, part, swapped))
        first = jnp.where(place[1] == 0, pairs[0], pairs[1])
        second = jnp.where(place[1] == 0, pairs[1], pairs[0])
        blocks += [first, second]
    sst[...] = jnp.concatenate(blocks, axis=0).astype(BF16)

    rows, rest = [], []
    for pair in range(CHUNKS // 2):
        tails = [
            mine[2 * pair + i, pl.ds(BIG, 16), :].astype(F32)
            + other[2 * pair + i, pl.ds(BIG, 16), :].astype(F32)
            for i in range(2)
        ]
        rows.append(jnp.concatenate([tail[:8] for tail in tails], axis=1))
        if pair < 10:
            rest.append(jnp.concatenate([tail[8:9] for tail in tails], axis=1))
    force_out[...] = jnp.concatenate(rows, axis=0).astype(BF16)
    conv_out[...] = jnp.concatenate(rest[:9], axis=0).astype(BF16)
    gain_out[...] = rest[9].astype(BF16).reshape(gain_out.shape)


def body(
    air,
    head,
    lat,
    drive,
    taps,
    gain,
    widen,
    shrink,
    thermal,
    sites,
    margin,
    water,
    adj,
):
    place = jnp.stack([lax.axis_index("core"), lax.axis_index("near")]).astype(jnp.int32)
    sites_t = jnp.transpose(sites, (0, 2, 1))
    margin_t = jnp.transpose(margin, (0, 2, 1))
    water_t = jnp.transpose(water)
    fluxes, to_left, to_right = call(
        start_kernel,
        (shape(32, 8, LINK), shape(HALO, CH), shape(HALO, CH)),
        [
            pltpu.VMEM((64, air.shape[-1]), BF16),
            pltpu.VMEM(head.shape, BF16),
            pltpu.VMEM((ROWS, OWN, CH), BF16),
            pltpu.VMEM((ROWS, OWN, CH), BF16),
            pltpu.VMEM((OWN, ROWS), jnp.int32),
            pltpu.VMEM((MARGINS, OWN, ROWS), jnp.int32),
            pltpu.VMEM((MARGINS, OWN, ROWS), jnp.int32),
            pltpu.SemaphoreType.DMA((7,)),
            pltpu.VMEM((80, LINK), F32),
            pltpu.VMEM((2 * CELLS, LINK), F32),
        ],
        limit=56,
        moved=2_000_000,
        far=range(7),
    )(air.reshape(64, -1), head, lat[0], adj[0], water_t, sites_t, margin_t)
    ring = [(i, (i + 1) % 32) for i in range(32)]
    left = lax.ppermute(to_right, TILE, ring)
    right = lax.ppermute(to_left, TILE, [(b, a) for a, b in ring])
    flux_in = lax.all_to_all(fluxes, TILE, 0, 0, tiled=True)
    gain_row = gain.reshape(1, CH)
    lat_own, cot, cot_t, sea, inverse, drive, taps, gain_row, spots = call(
        own_kernel,
        (
            held(CELLS, CH),
            held(CELLS, CH),
            held(CH, CELLS),
            held(CELLS, LINK),
            held(8, FARS, LINK, dtype=F32),
            held(LINK, CH),
            held(9, CH, dtype=F32),
            held(1, CH, dtype=F32),
            held(CELLS, 256),
        ),
        [
            pltpu.VMEM((ROWS, OWN, CH), BF16),
            pltpu.VMEM((ROWS, OWN, CH), BF16),
            pltpu.VMEM((OWN, ROWS), jnp.int32),
            pltpu.VMEM((MARGINS, OWN, ROWS), jnp.int32),
            pltpu.VMEM((MARGINS, OWN, ROWS), jnp.int32),
            pltpu.SemaphoreType.DMA((8,)),
            pltpu.VMEM((2 * CELLS, LINK), F32),
            pltpu.VMEM((ROWS, LINK), F32),
        ],
        moved=4_000_000,
        far=range(8),
    )(lat[0], adj[0], drive, taps, gain_row, water_t, sites_t, margin_t)
    keep, send, mixed, forcing, xhat, rstd, hidden, pre_cot, widen, shrink = call(
        ocean_kernel,
        (
            held(CHUNKS, BIG, LINK, dtype=F32),
            held(CHUNKS, BIG, LINK),
            held(2 * WIDE, PAD, LINK, dtype=F32),
            held(CELLS, LINK),
            held(MID * ROWS, CH, dtype=F32),
            held(MID * ROWS, LINK, dtype=F32),
            held(CELLS, HID),
            held(MID * ROWS, HID),
            held(CH, HID),
            held(HID, CH),
        ),
        [
            pltpu.SemaphoreType.DMA((2,)),
            pltpu.VMEM((MID * ROWS, CH), BF16),
            pltpu.VMEM((2, MID * ROWS, CH), F32),
            pltpu.VMEM((2, MID * ROWS, CH), F32),
            pltpu.VMEM((CH, HID), F32),
            pltpu.VMEM((HID, CH), F32),
        ],
        limit=24,
        flops=4_000_000_000,
        moved=10_000_000,
        smem=(0,),
        far=(11, 12),
    )(
        place,
        flux_in.reshape(256, LINK),
        spots,
        lat_own,
        left,
        right,
        cot,
        cot_t,
        drive,
        taps,
        gain_row,
        widen,
        shrink,
    )
    adj_turned, succ_turned, small = call(
        rest_kernel,
        (held(CELLS, CH), held(CELLS, CH), held(CHUNKS, 16, LINK, dtype=F32)),
        [
            pltpu.VMEM((2 * MID, PAD, LINK), F32),
            pltpu.VMEM((MID * ROWS, CH), F32),
        ],
        flops=1_000_000_000,
        moved=8_000_000,
    )(mixed, forcing, xhat, rstd, pre_cot, cot, taps, gain_row, widen, hidden, shrink, sea)

    swap = [(0, 1), (1, 0)]
    got = lax.ppermute(send, "core", swap)
    stage = call(core_sum_kernel, held(CHUNKS, CHUNK, LINK), moved=2_000_000)(keep, got, small)
    stage, succ_turned = lax.optimization_barrier((stage, succ_turned))
    stage = lax.all_to_all(stage, GROUP, 0, 0, tiled=True)
    succ, sst_near, sst_across, adj_out = call(
        state_kernel,
        (
            shape(ROWS, OWN, CH),
            held(2, 2, FARS, LINK),
            held(2, 2, FARS, LINK),
            shape(ROWS, OWN, CH),
        ),
        [
            pltpu.VMEM((CH, LINK), BF16),
            pltpu.SemaphoreType.DMA(()),
            pltpu.VMEM((2 * CELLS, LINK), F32),
            pltpu.VMEM((ROWS, LINK), F32),
        ],
        flops=1_000_000_000,
        moved=5_000_000,
        smem=(3,),
        far=(4,),
    )(succ_turned, inverse, adj_turned, place, thermal)
    across = lax.ppermute(sst_across, "core", swap)
    stage = call(group_sum_kernel, held(FARS, PIECE, LINK), moved=700_000)(stage, sst_near, across)
    stage = lax.all_to_all(stage, "far", 0, 0, tiled=True)
    cells = lax.axis_size(ENS) * lax.axis_size(TILE) * CELLS
    stage, surface = call(
        functools.partial(far_sum_kernel, 1.0 / math.sqrt(cells)),
        (held(CHUNKS, CHUNK, LINK), held(FARS, 16, LINK)),
        moved=700_000,
    )(stage)
    stage = lax.all_to_all(stage, GROUP, 0, 0, tiled=True)
    moved = lax.ppermute(surface, "near", swap)
    stage, moved = lax.optimization_barrier((stage, moved))
    other = lax.ppermute(stage, "core", swap)
    grad_up, grad_down, grad_force, grad_conv, grad_gain, sst_out = call(
        final_kernel,
        (
            shape(CH, HID),
            shape(HID, CH),
            shape(LINK, CH),
            shape(9, CH),
            shape(CH),
            shape(64, LINK),
        ),
        moved=2_000_000,
        smem=(0,),
    )(place, stage, other, surface, moved)
    return (
        succ[None],
        sst_out.reshape(1, 1, 64, LINK),
        adj_out[None],
        grad_force,
        grad_conv,
        grad_gain,
        grad_up,
        grad_down,
    )


def solution(mesh):
    finer = Mesh(mesh.devices.reshape(4, 4, 8, 2, 2), (*ENS, *TILE))
    return jax.shard_map(
        body,
        mesh=finer,
        in_specs=(
            P(ENS, TILE, None, None),
            P(),
            P(ENS, None, TILE, None),
            P(),
            P(),
            P(),
            P(),
            P(),
            P(),
            P(None, None, TILE),
            P(None, None, TILE),
            P(None, TILE),
            P(ENS, None, TILE, None),
        ),
        out_specs=(
            P(ENS, None, TILE, None),
            P(ENS, TILE, None, None),
            P(ENS, None, TILE, None),
            P(),
            P(),
            P(),
            P(),
            P(),
        ),
        check_vma=False,
    )
```

```python
import functools
import math

import jax
import jax.numpy as jnp
from jax import lax
from jax.experimental import pallas as pl
from jax.experimental.pallas import tpu as pltpu
from jax.sharding import Mesh
from jax.sharding import PartitionSpec as P

F32 = jnp.float32
BF16 = jnp.bfloat16
ENS = ("ens_0", "ens_1")
TILE = ("far", "near", "core")
GROUP = (*ENS, "near")

ROWS = 128
OWN = 8
CH = 256
HID = 1024
LINK = 128
MARGINS = 4
WIDE = OWN + 4
MID = OWN + 2
HALO = 3 * ROWS + 16
CHUNKS = 32
FARS = 8
BIG = 64
CHUNK = 80
BLOCK = 64
PIECE = 96
GELU_A = math.sqrt(2.0 / math.pi)
GELU_B = GELU_A * 0.044715


def call(kernel, out_shape, scratch=(), limit=16, flops=0, moved=0, smem=(), far=(), out_far=()):
    def run(*args):
        args = [
            pltpu.with_memory_space_constraint(arg, pltpu.HBM) if i in far else arg
            for i, arg in enumerate(args)
        ]

        def space(i):
            if i in smem:
                return pltpu.SMEM
            return pltpu.HBM if i in far else pltpu.VMEM

        return pl.pallas_call(
            kernel,
            out_shape=out_shape,
            in_specs=[pl.BlockSpec(memory_space=space(i)) for i in range(len(args))],
            out_specs=tuple(
                pl.BlockSpec(memory_space=pltpu.HBM if i in out_far else pltpu.VMEM)
                for i in range(len(out_shape))
            )
            if isinstance(out_shape, tuple)
            else pl.BlockSpec(memory_space=pltpu.VMEM),
            scratch_shapes=list(scratch),
            compiler_params=pltpu.CompilerParams(vmem_limit_bytes=limit * 2**20),
            cost_estimate=pl.CostEstimate(flops=flops, bytes_accessed=moved, transcendentals=0),
        )(*args)

    return run


def shape(*dims, dtype=BF16):
    return jax.ShapeDtypeStruct(dims, dtype)


def held(*dims, dtype=BF16):
    return pltpu.VMEM(dims, dtype)


def dot(a, b, contract=((1,), (0,))):
    return lax.dot_general(a, b, (contract, ((), ())), preferred_element_type=F32)


NT = ((1,), (1,))
TN = ((0,), (0,))


CELLS = ROWS * OWN


def put_rows(turned, value):
    flat = value.astype(F32).reshape(CELLS, CH)
    turned[pl.ds(0, CELLS), :] = flat[:, :128]
    turned[pl.ds(CELLS, CELLS), :] = flat[:, 128:]


def column(turned, c):
    low = turned[pl.ds(c, ROWS, stride=OWN), :]
    high = turned[pl.ds(CELLS + c, ROWS, stride=OWN), :]
    return jnp.concatenate([low, high], axis=1)


def put_column(turned, c, value):
    turned[pl.ds(c, ROWS, stride=OWN), :] = value[:, :128]
    turned[pl.ds(CELLS + c, ROWS, stride=OWN), :] = value[:, 128:]


def rows_of(turned):
    flat = jnp.concatenate([turned[pl.ds(0, CELLS), :], turned[pl.ds(CELLS, CELLS), :]], axis=1)
    return flat.reshape(ROWS, OWN, CH).astype(BF16)


def fetch(sources, targets, sems):
    copies = [
        pltpu.make_async_copy(source, target, sems.at[i])
        for i, (source, target) in enumerate(zip(sources, targets, strict=True))
    ]
    for copy in copies:
        copy.start()
    return copies


def sea_columns(water):
    eye = lax.broadcasted_iota(jnp.int32, (ROWS, ROWS), 0) == lax.broadcasted_iota(
        jnp.int32, (ROWS, ROWS), 1
    )
    ones = jnp.ones((ROWS, CH), BF16)
    wet = water[...].astype(F32)

    def one(c):
        spread = jnp.where(eye, jnp.broadcast_to(wet[c : c + 1], (ROWS, ROWS)), 0.0)
        return dot(spread.astype(BF16), ones)

    return one


def spots_of(ids, weight, shift):
    place = lax.broadcasted_iota(jnp.int32, (256, ROWS), 0)
    total = jnp.zeros((256, ROWS), F32)
    for k in range(MARGINS):
        spot = (ids[k] >> 1) * 8 + (ids[k] & 1) + shift
        total = total + jnp.where(place == spot, weight[k], 0.0)
    return jnp.transpose(total).astype(BF16)


def start_kernel(
    air_far,
    head_far,
    lat_far,
    adj_far,
    water_far,
    sites_far,
    margin_far,
    out,
    to_left,
    to_right,
    air,
    head,
    lat,
    adj,
    water,
    sites,
    margin,
    sems,
    wrapped,
    turned,
):
    copies = fetch(
        (air_far, head_far, lat_far, adj_far, water_far, sites_far, margin_far),
        (air, head, lat, adj, water, sites, margin),
        sems,
    )
    copies[0].wait()
    copies[1].wait()
    fluxes = dot(air[...], head[...])
    wrapped[pl.ds(8, 64), :] = fluxes
    wrapped[pl.ds(0, 8), :] = fluxes[56:64]
    wrapped[pl.ds(72, 8), :] = fluxes[0:8]
    for tile in range(32):
        out[tile] = wrapped[pl.ds(6 + 2 * tile, 8), :].astype(BF16)
    copies[2].wait()
    sides = ((to_left, 0, 0), (to_right, OWN - 2, OWN - 1))
    put_rows(turned, lat[...])
    for ref, first, edge in sides:
        for q in range(2):
            ref[pl.ds(q * ROWS, ROWS), :] = column(turned, first + q).astype(BF16)
    copies[3].wait()
    copies[4].wait()
    put_rows(turned, adj[...])
    sea = sea_columns(water)
    for ref, first, edge in sides:
        ref[pl.ds(2 * ROWS, ROWS), :] = (column(turned, edge) * sea(edge)).astype(BF16)
    copies[5].wait()
    copies[6].wait()
    for ref, first, edge in sides:
        ids = jnp.concatenate([sites[k, first : first + 2, :] for k in range(MARGINS)], axis=0)
        weights = jnp.concatenate([margin[k, first : first + 2, :] for k in range(MARGINS)], axis=0)
        packed = jnp.concatenate([ids, weights], axis=1).astype(F32)
        ref[pl.ds(3 * ROWS, 16), :] = jnp.concatenate(
            [packed, jnp.zeros_like(packed)], axis=0
        ).astype(BF16)


def own_kernel(
    lat_far,
    adj_far,
    drive_far,
    taps_far,
    gain_far,
    water_far,
    sites_far,
    margin_far,
    lat_out,
    cot_out,
    cot_t,
    sea_out,
    inverse,
    drive,
    taps,
    gain,
    spots,
    lat,
    adj,
    water,
    sites,
    margin,
    sems,
    turned,
    sums,
):
    copies = fetch(
        (sites_far, margin_far, water_far, lat_far, adj_far, drive_far, taps_far, gain_far),
        (sites, margin, water, lat, adj, drive, taps, gain),
        sems,
    )
    for copy in copies[:3]:
        copy.wait()
    for c in range(OWN):
        ids = [sites[k, c : c + 1, :] for k in range(MARGINS)]
        weight = [margin[k, c : c + 1, :].astype(F32) for k in range(MARGINS)]
        spots[pl.ds(c * ROWS, ROWS), :] = spots_of(ids, weight, 2)
    sea = sea_columns(water)
    masks = [sea(c) for c in range(OWN)]
    for c in range(OWN):
        sea_out[pl.ds(c * ROWS, ROWS), :] = masks[c][:, :LINK].astype(BF16)
    for half in range(2):
        sums[...] = sum(masks[half * 4 + c][:, :LINK] for c in range(4))
        for spot in range(4):
            count = sum(sums[pl.ds(4 * spot + i, FARS, stride=16), :] for i in range(4))
            inverse[4 * half + spot] = 1.0 / jnp.maximum(count, 1.0)
    copies[3].wait()
    put_rows(turned, lat[...])
    for c in range(OWN):
        lat_out[pl.ds(c * ROWS, ROWS), :] = column(turned, c).astype(BF16)
    copies[4].wait()
    put_rows(turned, adj[...])
    for c in range(OWN):
        cot = column(turned, c) * masks[c]
        cot_out[pl.ds(c * ROWS, ROWS), :] = cot.astype(BF16)
        cot_t[:, pl.ds(c * ROWS, ROWS)] = jnp.transpose(cot).astype(BF16)
    for copy in copies[5:]:
        copy.wait()


PAD = ROWS + 16


def clear_pads(ref):
    zeros = jnp.zeros((8, LINK), F32)
    for i in range(ref.shape[0]):
        ref[i, pl.ds(0, 8), :] = zeros
        ref[i, pl.ds(8 + ROWS, 8), :] = zeros


def ocean_kernel(
    place,
    flux,
    spots,
    lat,
    left,
    right,
    cot,
    cot_t,
    drive,
    taps,
    gain,
    widen_far,
    shrink_far,
    keep,
    send,
    mixed,
    forcing,
    xhat,
    rstd,
    hidden,
    states,
    pre_cot,
    widen,
    sems,
    shrink,
    normed,
    pres,
    cotangents,
    up,
    down,
):
    copies = fetch((widen_far, shrink_far), (widen, shrink), sems)
    clear_pads(mixed)
    outer = []
    for ref, shift in ((left, 0), (right, 4)):
        packed = ref[pl.ds(3 * ROWS, 16), :].astype(F32)
        for q in range(2):
            rows = [packed[2 * k + q : 2 * k + q + 1] for k in range(MARGINS)]
            ids = [row[:, :ROWS].astype(jnp.int32) for row in rows]
            outer.append(spots_of(ids, [row[:, ROWS:] for row in rows], shift))
    weights = jnp.concatenate([*outer[:2], spots[...], *outer[2:]], axis=0)
    source = jnp.concatenate([flux[...], jnp.ones((256, LINK), BF16)], axis=1)
    both = dot(weights, source)
    force = (both[:, :LINK] / both[:, LINK:]).astype(BF16)
    forcing[...] = force[2 * ROWS : 2 * ROWS + CELLS]
    pushed = dot(force, drive[...])
    for e in range(WIDE):
        if e < 2:
            state = left[pl.ds(e * ROWS, ROWS), :]
        elif e < 2 + OWN:
            state = lat[pl.ds((e - 2) * ROWS, ROWS), :]
        else:
            state = right[pl.ds((e - 2 - OWN) * ROWS, ROWS), :]
        value = state.astype(F32) + pushed[e * ROWS : (e + 1) * ROWS]
        value = value.astype(BF16).astype(F32)
        if 2 <= e < 2 + OWN:
            states[pl.ds((e - 2) * ROWS, ROWS), :] = value.astype(BF16)
        for h in range(2):
            mixed[2 * e + h, pl.ds(8, ROWS), :] = value[:, h * LINK : (h + 1) * LINK]
    tap = taps[...]
    scale = gain[...]

    def forward(n, carry):
        convs = []
        for h in range(2):
            total = None
            for a in range(3):
                for b in range(3):
                    part = (
                        tap[3 * a + b : 3 * a + b + 1, h * LINK : (h + 1) * LINK]
                        * mixed[2 * (n + b) + h, pl.ds(7 + a, ROWS), :]
                    )
                    total = part if total is None else total + part
            convs.append(total)
        mean = jnp.sum(convs[0] + convs[1], axis=1, keepdims=True) * (1.0 / CH)
        centred = [conv - mean for conv in convs]
        squares = centred[0] * centred[0] + centred[1] * centred[1]
        inv = lax.rsqrt(jnp.sum(squares, axis=1, keepdims=True) * (1.0 / CH) + 1e-6)
        hat = jnp.concatenate([c * inv for c in centred], axis=1)
        rows = pl.ds(pl.multiple_of(n * ROWS, ROWS), ROWS)
        xhat[rows, :] = hat
        rstd[rows, :] = jnp.broadcast_to(inv, (ROWS, LINK))
        normed[rows, :] = (hat * scale).astype(BF16)
        return carry

    lax.fori_loop(0, MID, forward, 0, unroll=MID)
    for copy in copies:
        copy.wait()
    norm = normed[...]
    norm_t = jnp.transpose(norm[ROWS : ROWS + CELLS])
    cots = jnp.concatenate(
        [left[pl.ds(2 * ROWS, ROWS), :], cot[...], right[pl.ds(2 * ROWS, ROWS), :]], axis=0
    )
    for j in range(4):
        cols = pl.ds(j * 256, 256)
        pres[j % 2] = dot(norm, widen[:, cols])
        cotangents[j % 2] = dot(cots, shrink[cols, :], NT)
        for first in range(0, MID * ROWS, BLOCK):
            rows = pl.ds(first, BLOCK)
            pre = pres[j % 2, rows, :]
            square = pre * pre
            bend = jnp.tanh(pre * (GELU_A + GELU_B * square))
            half = 0.5 * pre
            more = 1.0 + bend
            if ROWS <= first < ROWS + CELLS:
                hidden[pl.ds(first - ROWS, BLOCK), cols] = (half * more).astype(BF16)
            slope = 0.5 * more + half * (1.0 - bend * bend) * (GELU_A + 3.0 * GELU_B * square)
            pre_cot[rows, cols] = (cotangents[j % 2, rows, :] * slope).astype(BF16)
        up[:, cols] = dot(norm_t, pre_cot[pl.ds(ROWS, CELLS), cols])
        down[cols, :] = jnp.transpose(dot(cot_t[...], hidden[:, cols]))

    def pack(side, out):
        for g in range(CHUNKS):
            rows_up = pl.ds(side * 128 + g // 4 * 16, 16)
            rows_down = pl.ds(side * 512 + g * 16, 16)
            first = g % 4 * 256
            tiles = [up[rows_up, first : first + 128], up[rows_up, first + 128 : first + 256]]
            tiles += [down[rows_down, :128], down[rows_down, 128:]]
            out[g] = jnp.concatenate(tiles, axis=0).astype(out.dtype)

    for side in range(2):

        @pl.when(place[0] == side)
        def _():
            pack(side, keep)
            pack(1 - side, send)


def rest_kernel(
    mixed,
    forcing,
    xhat,
    rstd,
    pre_cot,
    cot,
    taps,
    gain,
    widen,
    adj_out,
    small,
    curve,
    back,
):
    clear_pads(curve)
    back[...] = dot(pre_cot[...], widen[...], NT)
    scale = gain[...]
    tap = taps[...]

    def backward(n, total):
        rows = pl.ds(pl.multiple_of(n * ROWS, ROWS), ROWS)
        normed_cot = back[rows, :]
        hat = xhat[rows, :]
        grown = normed_cot * scale
        mean = jnp.mean(grown, axis=1, keepdims=True)
        along = jnp.mean(grown * hat, axis=1, keepdims=True)
        inv = rstd[rows, :]
        for h in range(2):
            part = slice(h * LINK, (h + 1) * LINK)
            curve[2 * n + h, pl.ds(8, ROWS), :] = inv * (grown[:, part] - mean - hat[:, part] * along)
        inside = jnp.logical_and(n >= 1, n <= OWN)
        product = jnp.sum((normed_cot * hat).reshape(ROWS // 8, 8, CH), axis=0)
        return total + jnp.where(inside, product, 0.0)

    gain_sum = lax.fori_loop(
        0, MID, backward, jnp.zeros((8, CH), F32), unroll=MID
    )
    gain_grad = jnp.sum(gain_sum, axis=0, keepdims=True)

    def eightfold(x):
        return jnp.sum(x.reshape(ROWS // 8, 8, LINK), axis=0)

    tap_grads = [[jnp.zeros((8, LINK), F32) for _ in range(9)] for _ in range(2)]
    for c in range(OWN):
        halves = []
        for h in range(2):
            lanes = slice(h * LINK, (h + 1) * LINK)
            moved = [curve[2 * (c + 1) + h, pl.ds(9 - a, ROWS), :] for a in range(3)]
            around = [mixed[2 * (c + 1 + b) + h, pl.ds(8, ROWS), :] for b in range(3)]
            for a in range(3):
                for b in range(3):
                    tap_grads[h][3 * a + b] += eightfold(moved[a] * around[b])
            total = cot[pl.ds(c * ROWS, ROWS), lanes].astype(F32)
            for b in range(3):
                for a in range(3):
                    near = moved[a] if b == 1 else curve[2 * (c + 2 - b) + h, pl.ds(9 - a, ROWS), :]
                    total = total + tap[3 * a + b : 3 * a + b + 1, lanes] * near
            halves.append(total)
        value = jnp.concatenate(halves, axis=1).astype(BF16)
        adj_out[pl.ds(c * ROWS, ROWS), :] = value
    force_grad = dot(forcing[...], adj_out[...], TN)

    rest = jnp.concatenate(
        [
            jnp.concatenate(
                [jnp.sum(tap_grads[h][t], axis=0, keepdims=True) for h in range(2)], axis=1
            )
            for t in range(9)
        ]
        + [gain_grad],
        axis=0,
    )
    for g in range(CHUNKS):
        lanes = slice(g % 2 * 128, g % 2 * 128 + 128)
        tail = jnp.zeros((8, LINK), F32)
        if g < 20:
            tail = jnp.concatenate([rest[g // 2 : g // 2 + 1, lanes], tail[1:]], axis=0)
        small[g] = jnp.concatenate([force_grad[g // 2 * 8 : g // 2 * 8 + 8, lanes], tail], axis=0)


def state_kernel(
    hidden_far,
    states_far,
    shrink_far,
    thermal_far,
    sea,
    inverse,
    adj,
    place,
    succ_out,
    sst_near,
    sst_across,
    adj_out,
    hidden,
    states,
    shrink,
    thermal,
    sems,
    turned,
    sums,
):
    copies = fetch(
        (shrink_far, hidden_far, states_far, thermal_far), (shrink, hidden, states, thermal), sems
    )
    for c in range(OWN):
        put_column(turned, c, adj[pl.ds(c * ROWS, ROWS), :].astype(F32))
    adj_out[...] = rows_of(turned)
    for copy in copies:
        copy.wait()
    mlp = dot(hidden[...], shrink[...])
    fine = [None, None]
    for c in range(OWN):
        rows = slice(c * ROWS, (c + 1) * ROWS)
        mask = sea[rows, :].astype(F32)
        mask = jnp.concatenate([mask, mask], axis=1)
        value = (mask * (states[rows, :].astype(F32) + mlp[rows])).astype(BF16)
        put_column(turned, c, value.astype(F32))
        part = dot(value, thermal[...])
        fine[c // 4] = part if c % 4 == 0 else fine[c // 4] + part
    succ_out[...] = rows_of(turned)
    for half in range(2):
        sums[...] = fine[half]
        for across, out in enumerate((sst_near, sst_across)):
            for other in range(2):
                core = jnp.bitwise_xor(place[0], across)
                spot = 2 * jnp.bitwise_xor(place[1], other) + core
                coarse = sum(sums[pl.ds(4 * spot + i, FARS, stride=16), :] for i in range(4))
                out[other, half] = (coarse * inverse[4 * half + spot]).astype(BF16)


def core_sum_kernel(keep, got, small, out):
    for g in range(CHUNKS):
        out[g, pl.ds(0, BIG), :] = (keep[g] + got[g].astype(F32)).astype(BF16)
        out[g, pl.ds(BIG, 16), :] = small[g].astype(BF16)


def group_sum_kernel(got, near, across, out):
    total = got[0].astype(F32)
    for g in range(1, CHUNKS):
        total = total + got[g].astype(F32)
    value = total.astype(BF16)
    row = lax.broadcasted_iota(jnp.int32, (8, LINK), 0)
    surface = [ref[i, half].astype(F32) for i in range(2) for ref in (near, across) for half in range(2)]
    for far in range(FARS):
        lower = jnp.broadcast_to(surface[0][far : far + 1], (8, LINK))
        for i in range(1, 8):
            lower = jnp.where(row == i, jnp.broadcast_to(surface[i][far : far + 1], (8, LINK)), lower)
        out[far, pl.ds(0, CHUNK), :] = value
        out[far, pl.ds(CHUNK, 16), :] = jnp.concatenate([lower, lower], axis=0).astype(BF16)


def far_sum_kernel(factor, got, out, surface):
    total = got[0, pl.ds(0, CHUNK), :].astype(F32)
    for far in range(1, FARS):
        total = total + got[far, pl.ds(0, CHUNK), :].astype(F32)
    value = (total * factor).astype(BF16)
    for g in range(CHUNKS):
        out[g] = value
    for far in range(FARS):
        surface[far] = got[far, pl.ds(CHUNK, 16), :]


def final_kernel(place, mine, other, kept, moved, up_out, down_out, force_out, conv_out, gain_out, sst):
    def unpack(side, ref):
        for row in range(8):
            tiles = [ref[4 * row + i, pl.ds(t * 16, 16), :] for i in range(4) for t in range(2)]
            up_out[pl.ds(side * 128 + row * 16, 16), :] = jnp.concatenate(tiles, axis=1)
        for g in range(CHUNKS):
            tiles = [ref[g, pl.ds(32 + t * 16, 16), :] for t in range(2)]
            down_out[pl.ds(side * 512 + g * 16, 16), :] = jnp.concatenate(tiles, axis=1)

    for side in range(2):

        @pl.when(place[0] == side)
        def _():
            unpack(side, mine)
            unpack(1 - side, other)

    blocks = []
    for far in range(FARS):
        own, came = kept[far].astype(F32)[0:4], moved[far].astype(F32)[4:8]
        pairs = []
        for part in (own, came):
            swapped = jnp.concatenate([part[2:4], part[0:2]], axis=0)
            pairs.append(jnp.where(place[0] == 0, part, swapped))
        first = jnp.where(place[1] == 0, pairs[0], pairs[1])
        second = jnp.where(place[1] == 0, pairs[1], pairs[0])
        blocks += [first, second]
    sst[...] = jnp.concatenate(blocks, axis=0).astype(BF16)

    rows, rest = [], []
    for pair in range(CHUNKS // 2):
        tails = [
            mine[2 * pair + i, pl.ds(BIG, 16), :].astype(F32)
            + other[2 * pair + i, pl.ds(BIG, 16), :].astype(F32)
            for i in range(2)
        ]
        rows.append(jnp.concatenate([tail[:8] for tail in tails], axis=1))
        if pair < 10:
            rest.append(jnp.concatenate([tail[8:9] for tail in tails], axis=1))
    force_out[...] = jnp.concatenate(rows, axis=0).astype(BF16)
    conv_out[...] = jnp.concatenate(rest[:9], axis=0).astype(BF16)
    gain_out[...] = rest[9].astype(BF16).reshape(gain_out.shape)


def body(
    air,
    head,
    lat,
    drive,
    taps,
    gain,
    widen,
    shrink,
    thermal,
    sites,
    margin,
    water,
    adj,
):
    place = jnp.stack([lax.axis_index("core"), lax.axis_index("near")]).astype(jnp.int32)
    sites_t = jnp.transpose(sites, (0, 2, 1))
    margin_t = jnp.transpose(margin, (0, 2, 1))
    water_t = jnp.transpose(water)
    fluxes, to_left, to_right = call(
        start_kernel,
        (shape(32, 8, LINK), shape(HALO, CH), shape(HALO, CH)),
        [
            pltpu.VMEM((64, air.shape[-1]), BF16),
            pltpu.VMEM(head.shape, BF16),
            pltpu.VMEM((ROWS, OWN, CH), BF16),
            pltpu.VMEM((ROWS, OWN, CH), BF16),
            pltpu.VMEM((OWN, ROWS), jnp.int32),
            pltpu.VMEM((MARGINS, OWN, ROWS), jnp.int32),
            pltpu.VMEM((MARGINS, OWN, ROWS), jnp.int32),
            pltpu.SemaphoreType.DMA((7,)),
            pltpu.VMEM((80, LINK), F32),
            pltpu.VMEM((2 * CELLS, LINK), F32),
        ],
        limit=56,
        moved=2_000_000,
        far=range(7),
    )(air.reshape(64, -1), head, lat[0], adj[0], water_t, sites_t, margin_t)
    ring = [(i, (i + 1) % 32) for i in range(32)]
    left = lax.ppermute(to_right, TILE, ring)
    right = lax.ppermute(to_left, TILE, [(b, a) for a, b in ring])
    flux_in = lax.all_to_all(fluxes, TILE, 0, 0, tiled=True)
    gain_row = gain.reshape(1, CH)
    lat_own, cot, cot_t, sea, inverse, drive, taps, gain_row, spots = call(
        own_kernel,
        (
            held(CELLS, CH),
            held(CELLS, CH),
            held(CH, CELLS),
            held(CELLS, LINK),
            held(8, FARS, LINK, dtype=F32),
            held(LINK, CH),
            held(9, CH, dtype=F32),
            held(1, CH, dtype=F32),
            held(CELLS, 256),
        ),
        [
            pltpu.VMEM((ROWS, OWN, CH), BF16),
            pltpu.VMEM((ROWS, OWN, CH), BF16),
            pltpu.VMEM((OWN, ROWS), jnp.int32),
            pltpu.VMEM((MARGINS, OWN, ROWS), jnp.int32),
            pltpu.VMEM((MARGINS, OWN, ROWS), jnp.int32),
            pltpu.SemaphoreType.DMA((8,)),
            pltpu.VMEM((2 * CELLS, LINK), F32),
            pltpu.VMEM((ROWS, LINK), F32),
        ],
        moved=4_000_000,
        far=range(8),
    )(lat[0], adj[0], drive, taps, gain_row, water_t, sites_t, margin_t)
    keep, send, mixed, forcing, xhat, rstd, hidden, states, pre_cot, widen = call(
        ocean_kernel,
        (
            held(CHUNKS, BIG, LINK, dtype=F32),
            held(CHUNKS, BIG, LINK),
            held(2 * WIDE, PAD, LINK, dtype=F32),
            held(CELLS, LINK),
            held(MID * ROWS, CH, dtype=F32),
            held(MID * ROWS, LINK, dtype=F32),
            held(CELLS, HID),
            held(CELLS, CH),
            held(MID * ROWS, HID),
            held(CH, HID),
        ),
        [
            pltpu.SemaphoreType.DMA((2,)),
            pltpu.VMEM((HID, CH), BF16),
            pltpu.VMEM((MID * ROWS, CH), BF16),
            pltpu.VMEM((2, MID * ROWS, CH), F32),
            pltpu.VMEM((2, MID * ROWS, CH), F32),
            pltpu.VMEM((CH, HID), F32),
            pltpu.VMEM((HID, CH), F32),
        ],
        limit=24,
        flops=4_000_000_000,
        moved=10_000_000,
        smem=(0,),
        far=(11, 12),
    )(
        place,
        flux_in.reshape(256, LINK),
        spots,
        lat_own,
        left,
        right,
        cot,
        cot_t,
        drive,
        taps,
        gain_row,
        widen,
        shrink,
    )
    adj_turned, small = call(
        rest_kernel,
        (held(CELLS, CH), held(CHUNKS, 16, LINK, dtype=F32)),
        [
            pltpu.VMEM((2 * MID, PAD, LINK), F32),
            pltpu.VMEM((MID * ROWS, CH), F32),
        ],
        flops=1_000_000_000,
        moved=8_000_000,
    )(mixed, forcing, xhat, rstd, pre_cot, cot, taps, gain_row, widen)

    swap = [(0, 1), (1, 0)]
    got = lax.ppermute(send, "core", swap)
    stage = call(core_sum_kernel, held(CHUNKS, CHUNK, LINK), moved=2_000_000)(keep, got, small)
    stage, hidden, adj_turned = lax.optimization_barrier((stage, hidden, adj_turned))
    stage = lax.all_to_all(stage, GROUP, 0, 0, tiled=True)
    succ, sst_near, sst_across, adj_out = call(
        state_kernel,
        (
            shape(ROWS, OWN, CH),
            held(2, 2, FARS, LINK),
            held(2, 2, FARS, LINK),
            shape(ROWS, OWN, CH),
        ),
        [
            pltpu.VMEM((CELLS, HID), BF16),
            pltpu.VMEM((CELLS, CH), BF16),
            pltpu.VMEM((HID, CH), BF16),
            pltpu.VMEM((CH, LINK), BF16),
            pltpu.SemaphoreType.DMA((4,)),
            pltpu.VMEM((2 * CELLS, LINK), F32),
            pltpu.VMEM((ROWS, LINK), F32),
        ],
        flops=1_000_000_000,
        moved=5_000_000,
        smem=(7,),
        far=range(4),
    )(hidden, states, shrink, thermal, sea, inverse, adj_turned, place)
    across = lax.ppermute(sst_across, "core", swap)
    stage = call(group_sum_kernel, held(FARS, PIECE, LINK), moved=700_000)(stage, sst_near, across)
    stage = lax.all_to_all(stage, "far", 0, 0, tiled=True)
    cells = lax.axis_size(ENS) * lax.axis_size(TILE) * CELLS
    stage, surface = call(
        functools.partial(far_sum_kernel, 1.0 / math.sqrt(cells)),
        (held(CHUNKS, CHUNK, LINK), held(FARS, 16, LINK)),
        moved=700_000,
    )(stage)
    stage = lax.all_to_all(stage, GROUP, 0, 0, tiled=True)
    moved = lax.ppermute(surface, "near", swap)
    stage, moved = lax.optimization_barrier((stage, moved))
    other = lax.ppermute(stage, "core", swap)
    grad_up, grad_down, grad_force, grad_conv, grad_gain, sst_out = call(
        final_kernel,
        (
            shape(CH, HID),
            shape(HID, CH),
            shape(LINK, CH),
            shape(9, CH),
            shape(CH),
            shape(64, LINK),
        ),
        moved=2_000_000,
        smem=(0,),
    )(place, stage, other, surface, moved)
    return (
        succ[None],
        sst_out.reshape(1, 1, 64, LINK),
        adj_out[None],
        grad_force,
        grad_conv,
        grad_gain,
        grad_up,
        grad_down,
    )


def solution(mesh):
    finer = Mesh(mesh.devices.reshape(4, 4, 8, 2, 2), (*ENS, *TILE))
    return jax.shard_map(
        body,
        mesh=finer,
        in_specs=(
            P(ENS, TILE, None, None),
            P(),
            P(ENS, None, TILE, None),
            P(),
            P(),
            P(),
            P(),
            P(),
            P(),
            P(None, None, TILE),
            P(None, None, TILE),
            P(None, TILE),
            P(ENS, None, TILE, None),
        ),
        out_specs=(
            P(ENS, None, TILE, None),
            P(ENS, TILE, None, None),
            P(ENS, None, TILE, None),
            P(),
            P(),
            P(),
            P(),
            P(),
        ),
        check_vma=False,
    )
```
